512 devices in a mesh: grp: 4 (over x), gx: 128 (over z, y, core).
Axes of the slice: x: 4, y: 4, z: 16, core: 2. Of those that a mesh axis runs over, the one named last changes fastest.
Arguments:
- fourier: bfloat16 [128, 2, 16, 2560], P(None, None, 'grp', 'gx'), may hold values from -6 to 6
- lat_of_row: int32 [2560], replicated, may hold values from 0 to 2559, each once
- wave_order: int32 [128], replicated, may hold values from 0 to 127, each once
- analysis: bfloat16 [128, 128, 1280], P('gx'), may hold values from -0.125 to 0.125
- synthesis: bfloat16 [128, 1024, 128], P('gx'), may hold values from -0.046875 to 0.046875
- bracket: int32 [8, 1024, 3600], P(None, 'gx', 'grp'), may hold values from 0 to 14
- frac: float32 [8, 1024, 3600], P(None, 'gx', 'grp'), may hold values from 0 to 1
Outputs:
- pressure_field: float32 [8, 1024, 3600], P(None, 'gx', 'grp')
The draws below stay inside these ranges and needn't reach their ends.
Inputs may be any that keep to these rules, and one draw needn't show every extreme that they name: `lat_of_row`: each latitude index appears once. `wave_order`: each window index appears once.
All inputs are finite; a program needn't handle non-finite values.
Results may differ from the reference program's by a relative error of at most 0.0046.
Values may be sent and summed in bfloat16 or wider, within the bound.
A program may use at most 64 MiB of HBM per device.

```python
import math
import jax
import jax.numpy as jnp
from jax import lax

MTOT = 1280
NLAT = 2560
NLON = 3600
REG_DEV = 8
POUT = 8
LEV = 16
M_WIN = 128
NLATH = 1280
NREG = 1024
N_GX = 128


def place_ends(entries, key, least, high):
    longest = entries.shape.index(max(entries.shape))
    spots = []
    for shift in (0, 1):
        where = [jax.random.randint(jax.random.fold_in(key, axis), (), 0, length) for axis, length in enumerate(entries.shape)]
        where[longest] = (where[longest] + shift) % entries.shape[longest]
        spots.append(tuple(where))
    return entries.at[spots[0]].set(least).at[spots[1]].set(high)


def shard_levels(stream_key, shape, cuts, low, top_value):
    factor_of, own = 1.0, jax.random.fold_in(stream_key, 6)
    for position, parts in cuts:
        steps = jnp.exp(jax.random.uniform(jax.random.fold_in(own, position), (parts,), jnp.float32, low / len(cuts), top_value / len(cuts)))
        factor_of = factor_of * jnp.repeat(steps, shape[position] // parts).reshape([-1 if axis == position else 1 for axis in range(len(shape))])
    return factor_of


def centred(key, dims, scale, reach, shards=(), kind=jnp.bfloat16):
    array = jax.random.normal(key, dims, jnp.float32) * scale
    if len(shards) > 0:
        array = shard_levels(key, dims, shards, -0.22, 0.18) * array
    return jnp.clip(array, min=-reach, max=reach).astype(kind)


def setup_inputs(seed: int = 0) -> dict:
    keys = jax.random.split(jax.random.key(seed), 8)
    fourier = centred(keys[0], (M_WIN, 2, LEV, NLAT), 1.0, 6.0, ((2, 4), (3, 128)))
    lat_of_row = jax.random.permutation(keys[1], NLAT).astype(jnp.int32)
    wave_order = jax.random.permutation(keys[2], M_WIN).astype(jnp.int32)
    analysis = centred(keys[3], (M_WIN, M_WIN, NLATH), NLAT ** -0.5, 0.125, ((0, 128),))
    synthesis = centred(keys[4], (M_WIN, NREG, M_WIN), (M_WIN * M_WIN) ** -0.5, 0.046875, ((0, 128),))
    bracket = place_ends(jax.random.randint(keys[5], (POUT, NREG, NLON), 0, LEV - 1), jax.random.fold_in(keys[5], 1), 0, (LEV - 1) - 1).astype(jnp.int32)
    frac = jnp.clip(1.0 * jax.random.uniform(keys[6], (POUT, NREG, NLON), jnp.float32) ** shard_levels(keys[6], (POUT, NREG, NLON), ((1, 128), (2, 4)), -0.2, 0.2), 0.0, 1.0)
    return {"fourier": fourier, "lat_of_row": lat_of_row, "wave_order": wave_order, "analysis": analysis, "synthesis": synthesis, "bracket": bracket, "frac": frac}


def inverse_table(wave_order, lon_start, count):
    wave_m = MTOT - M_WIN + wave_order
    lons = lon_start + jnp.arange(count, dtype=jnp.int32)
    phase = (wave_m[:, None] * lons[None, :]) % NLON
    angle = phase.astype(jnp.float32) * (2.0 * math.pi / NLON)
    return jnp.stack([2.0 * jnp.cos(angle), -2.0 * jnp.sin(angle)], axis=1).astype(jnp.bfloat16)


def reference(fourier, lat_of_row, wave_order, analysis, synthesis, bracket, frac):
    pole = jnp.minimum(lat_of_row, NLAT - 1 - lat_of_row)
    loop_len = 20 + 4 * pole
    wave_m = MTOT - M_WIN + jnp.arange(M_WIN, dtype=jnp.int32)
    live = 2 * wave_m[:, None] < loop_len[None, :]
    masked = jnp.where(live[:, None, None, :], fourier, jnp.zeros((), fourier.dtype))
    ordered = jnp.take(masked, wave_order, axis=0)
    row_of_lat = jnp.zeros((NLAT,), jnp.int32).at[lat_of_row].set(jnp.arange(NLAT, dtype=jnp.int32))
    loops = jnp.take(ordered, row_of_lat, axis=3)
    north = loops[..., :NLATH].astype(jnp.float32)
    south = jnp.flip(loops[..., NLATH:], axis=3).astype(jnp.float32)
    table_an = analysis.astype(jnp.float32)
    from_north = jnp.einsum("celj,ckj->celk", north, table_an)
    from_south = jnp.einsum("celj,ckj->celk", south, table_an)
    degree = jnp.arange(M_WIN, dtype=jnp.int32)
    parity = jnp.where(degree % 2 == 0, 1.0, -1.0).astype(jnp.float32)
    keep = degree[None, :] < (M_WIN - wave_order)[:, None]
    spec = jnp.where(keep[:, None, None, :], from_north + parity * from_south, 0.0).astype(jnp.bfloat16)
    grid_four = jnp.einsum("celk,crk->celr", spec.astype(jnp.float32), synthesis.astype(jnp.float32)).astype(jnp.bfloat16)
    table = inverse_table(wave_order, 0, NLON).astype(jnp.float32)

    def block(number):
        start = number * REG_DEV
        piece = lax.dynamic_slice_in_dim(grid_four, start, REG_DEV, 3).astype(jnp.float32)
        field = jnp.einsum("celr,cen->lrn", piece, table)
        low_level = lax.dynamic_slice_in_dim(bracket, start, REG_DEV, 1)
        weight = lax.dynamic_slice_in_dim(frac, start, REG_DEV, 1)
        lower = jnp.take_along_axis(field, low_level, axis=0)
        upper = jnp.take_along_axis(field, low_level + 1, axis=0)
        return (1.0 - weight) * lower + weight * upper

    blocks = lax.map(block, jnp.arange(N_GX, dtype=jnp.int32))
    return jnp.transpose(blocks, (1, 0, 2, 3)).reshape(POUT, NREG, NLON)
```

```python
import functools
import math

import jax
import jax.numpy as jnp
from jax import lax
from jax.experimental import pallas as pl
from jax.experimental.pallas import tpu as pltpu
from jax.sharding import PartitionSpec as P

MESH = pl.DeviceIdType.MESH
F32, BF16, I32 = jnp.float32, jnp.bfloat16, jnp.int32

NX, NZ, NYC = 4, 16, 8
NGX = NZ * NYC
MTOT, NLAT, NLON = 1280, 2560, 3600
WAVES = 128
FIRST_WAVE = MTOT - WAVES
LEV_DEV, ROWS_DEV, LOOPS_DEV, LON_DEV, POUT, LEV = 4, 8, 20, 900, 8, 16
HALF = NLAT // 2
LANES = 128
LON_PAD = 1024


def iota(shape, axis):
    return lax.broadcasted_iota(I32, shape, axis)


def nt_dot(a, b):
    return lax.dot_general(a, b, (((1,), (1,)), ((), ())), preferred_element_type=F32)


def nn_dot(a, b):
    return lax.dot_general(a, b, (((1,), (0,)), ((), ())), preferred_element_type=F32)


def slot_source(shape):
    lane = iota(shape, 1)
    return (lane & (NZ - 1)) * NYC + (lane >> 4)


def ordered_waves(fourier, wave):
    pick = (iota((WAVES, WAVES), 0) == wave).astype(F32)
    pick = pick.T.astype(BF16)
    rows = jnp.concatenate([fourier[0].astype(F32), fourier[1].astype(F32)], axis=1)
    rows = rows.reshape(LOOPS_DEV * 8, WAVES)
    rows = jnp.concatenate([rows, jnp.zeros((256 - LOOPS_DEV * 8, WAVES), F32)], axis=0)
    return nt_dot(pick, rows.astype(BF16))


def loop_lats(lat):
    flat = slot_source((24, LANES)) * LOOPS_DEV + jnp.minimum(iota((24, LANES), 0), LOOPS_DEV - 1)
    high, low = flat >> 7, flat & (LANES - 1)
    out = jnp.zeros((24, LANES), I32)
    for a in range(LOOPS_DEV):
        row = jnp.broadcast_to(lat[a : a + 1], (24, LANES))
        out = jnp.where(high == a, jnp.take_along_axis(row, low, axis=1), out)
    return out


def table_tile(wave_col, lon):
    turns = wave_col * lon
    quarter = jnp.floor(turns.astype(F32) * (4.0 / NLON) + 0.5).astype(I32)
    rest = (turns - quarter * (NLON // 4)).astype(F32) * (2.0 * math.pi / NLON)
    sq = rest * rest
    c = 1.0 + sq * (-0.5 + sq * (1.0 / 24 + sq * (-1.0 / 720 + sq * (1.0 / 40320))))
    s = rest * (1.0 + sq * (-1.0 / 6 + sq * (1.0 / 120 + sq * (-1.0 / 5040 + sq * (1.0 / 362880)))))
    odd = (quarter & 1) == 1
    cos = jnp.where(odd, s, c)
    sin = jnp.where(odd, c, s)
    cos = jnp.where(((quarter + 1) & 2) == 2, -2.0 * cos, 2.0 * cos)
    sin = jnp.where((quarter & 2) == 2, 2.0 * sin, -2.0 * sin)
    return cos.astype(BF16), sin.astype(BF16)


def kernel(
    lat_ref, wave_ref, fourier_ref, analysis_ref, synthesis_ref, bracket_ref, frac_ref,
    out_ref,
    fourier_v, analysis_v, synthesis_v, bracket_v, frac_v,
    send1, recv1, send2, recv2, send3, recv3, send4, recv4,
    lats_s, sorted_s, spread_s, rows_s, syn_f, syn_s, wave_s, table_s, field_s,
    local_sem, send_sem, recv_sem,
):
    x = lax.axis_index("grp")
    gx = lax.axis_index("gx")
    z, yc = lax.div(gx, NYC), lax.rem(gx, NYC)

    local = [
        pltpu.make_async_copy(src, dst, local_sem.at[i])
        for i, (src, dst) in enumerate(
            (
                (fourier_ref, fourier_v),
                (analysis_ref, analysis_v),
                (synthesis_ref, synthesis_v),
                (bracket_ref, bracket_v),
                (frac_ref, frac_v),
            )
        )
    ]
    for copy in local:
        copy.start()

    barrier = pltpu.get_barrier_semaphore()

    @pl.loop(1, NZ)
    def _(d):
        pl.semaphore_signal(
            barrier, inc=1, device_id=(x, lax.rem(z + d, NZ) * NYC + yc), device_id_type=MESH
        )

    @pl.loop(1, NX * NYC)
    def _(d):
        tx = lax.rem(x + lax.div(d, NYC), NX)
        ty = lax.rem(yc + lax.rem(d, NYC), NYC)
        pl.semaphore_signal(barrier, inc=1, device_id=(tx, z * NYC + ty), device_id_type=MESH)

    def exchange_z(send, recv, stage):
        pltpu.make_async_copy(send.at[z], recv.at[z], recv_sem.at[stage]).start()

        @pl.loop(1, NZ)
        def _(d):
            tz = lax.rem(z + d, NZ)
            pltpu.make_async_remote_copy(
                src_ref=send.at[tz],
                dst_ref=recv.at[z],
                send_sem=send_sem.at[stage],
                recv_sem=recv_sem.at[stage],
                device_id=(x, tz * NYC + yc),
                device_id_type=MESH,
            ).start()

    def wait_all(ref, sem):
        pltpu.make_async_copy(ref, ref, sem).wait()

    wave = wave_ref[...]
    local[0].wait()
    ordered = ordered_waves(fourier_v[...], wave)
    head = ordered[:, :LANES].reshape(NZ, NYC, LANES)
    tail = ordered[:, LANES:].reshape(NZ, NYC, LANES)
    send1[...] = jnp.concatenate([head, tail], axis=1).astype(BF16)
    pl.semaphore_wait(barrier, NZ - 1 + NX * NYC - 1)
    exchange_z(send1, recv1, 0)

    lats = loop_lats(lat_ref[...])
    own = jnp.sum(jnp.where(iota((1, WAVES), 1) == gx, wave, 0), axis=1, keepdims=True)
    pole = jnp.minimum(lats, NLAT - 1 - lats)
    live = 2 * (FIRST_WAVE + own) < 20 + 4 * pole
    lats_s[0] = jnp.where(live, pole, -1)
    lats_s[1] = jnp.where(lats >= HALF, 1, 0)
    local[1].wait()

    def sort_pair(pair):
        row = lats_s[0, pl.ds(2 * pair, 2), :]
        south = lats_s[1, pl.ds(2 * pair, 2), :]
        row = jnp.concatenate([row[0:1], row[1:2]], axis=1)
        south = jnp.concatenate([south[0:1], south[1:2]], axis=1)
        total = jnp.zeros((WAVES, 2 * LANES), F32)
        for j in range(0, HALF, 256):
            hot = (iota((256, 2 * LANES), 0) + j == row).astype(F32).astype(BF16)
            total += nn_dot(analysis_v[:, j : j + 256], hot)
        odd = iota((WAVES, 2 * LANES), 0) & 1
        total = jnp.where((odd * south) == 1, -total, total)
        sorted_s[:, pl.ds(pl.multiple_of(pair * 256, 256), 256)] = total.astype(BF16)

    pl.loop(0, LOOPS_DEV // 4)(sort_pair)

    wait_all(recv1, recv_sem.at[0])
    spread_s[...] = recv1[...].astype(F32).reshape(NZ * 16, LANES)
    for ty in range(NYC):
        send2[ty, :, :LANES] = spread_s[pl.ds(ty, NZ, stride=16), :].astype(BF16)
        send2[ty, :, LANES:] = spread_s[pl.ds(8 + ty, NZ, stride=16), :].astype(BF16)
    pltpu.make_async_copy(send2.at[yc], recv2.at[yc], recv_sem.at[1]).start()

    @pl.loop(1, NYC)
    def _(d):
        ty = lax.rem(yc + d, NYC)
        pltpu.make_async_remote_copy(
            src_ref=send2.at[ty],
            dst_ref=recv2.at[yc],
            send_sem=send_sem.at[1],
            recv_sem=recv_sem.at[1],
            device_id=(x, z * NYC + ty),
            device_id_type=MESH,
        ).start()

    pl.loop(LOOPS_DEV // 4, LOOPS_DEV // 2)(sort_pair)
    local[2].wait()
    syn_f[...] = synthesis_v[...].astype(F32)
    for ri in range(ROWS_DEV):
        syn_s[:, ri * LANES : (ri + 1) * LANES] = syn_f[pl.ds(ri, NGX, stride=ROWS_DEV), :].astype(BF16)

    wait_all(recv2, recv_sem.at[1])
    loops = recv2[...].reshape(NGX, 2 * LANES).astype(F32)
    loops = jnp.concatenate([loops[:, :LANES].T, loops[:, LANES:].T], axis=0)
    loops = jnp.concatenate([loops[8 * s : 8 * s + 8] for s in range(LOOPS_DEV)], axis=1)
    spec = nt_dot(loops.astype(BF16), sorted_s[...])
    spec = jnp.where(iota((8, WAVES), 1) < WAVES - own, spec, 0.0).astype(BF16).astype(F32)
    wide = jnp.broadcast_to(spec[:, None, :], (8, ROWS_DEV, WAVES)).reshape(8 * ROWS_DEV, WAVES)
    ri = iota((8 * ROWS_DEV, WAVES), 0) & (ROWS_DEV - 1)
    wide = jnp.concatenate([jnp.where(ri == r, wide, 0.0) for r in range(ROWS_DEV)], axis=1)
    wide = jnp.concatenate([wide, jnp.zeros_like(wide)], axis=0).astype(BF16)
    rows = nt_dot(syn_s[...], wide)
    send3[...] = rows.reshape(NZ, NYC, LANES).astype(BF16)

    exchange_z(send3, recv3, 2)
    lane = iota((1, WAVES), 1)
    source = jnp.broadcast_to((lane & (NZ - 1)) * NYC + (lane >> 4), (8, WAVES))
    waves = jnp.take_along_axis(jnp.broadcast_to(wave, (8, WAVES)), source, axis=1)
    waves = jnp.broadcast_to(waves[0:1].astype(F32), (WAVES, WAVES)).T
    wave_s[...] = waves.astype(I32) + FIRST_WAVE
    lon_start = x * LON_DEV

    def table_rows(i):
        at = pl.ds(pl.multiple_of(i * 16, 16), 16)
        col = wave_s[at, :]
        for n in range(0, LON_PAD, LANES):
            lon = iota((16, LANES), 1) + (lon_start + n)
            cos, sin = table_tile(col, lon)
            table_s[0, at, n : n + LANES] = cos
            table_s[1, at, n : n + LANES] = sin

    pl.loop(0, 4)(table_rows)

    wait_all(recv3, recv_sem.at[2])
    rows_s[...] = recv3[...].astype(F32).reshape(NGX, LANES)
    for ty in range(NYC):
        send4[ty] = rows_s[pl.ds(ty, NZ, stride=NYC), :].astype(BF16)
    pltpu.make_async_copy(send4.at[yc], recv4.at[x, yc], recv_sem.at[3]).start()

    @pl.loop(1, NX * NYC)
    def _(d):
        tx = lax.rem(x + lax.div(d, NYC), NX)
        ty = lax.rem(yc + lax.rem(d, NYC), NYC)
        pltpu.make_async_remote_copy(
            src_ref=send4.at[ty],
            dst_ref=recv4.at[x, yc],
            send_sem=send_sem.at[3],
            recv_sem=recv_sem.at[3],
            device_id=(tx, z * NYC + ty),
            device_id_type=MESH,
        ).start()

    pl.loop(4, 8)(table_rows)

    wait_all(recv4, recv_sem.at[3])
    parts = []
    for tx in range(NX):
        block = recv4[tx].reshape(NGX, LANES).astype(F32).T
        parts.append(jnp.concatenate([block[0:32], block[32:64]], axis=1))
    rows = jnp.concatenate(parts, axis=0).astype(BF16)
    field = nn_dot(rows, table_s[...].reshape(2 * NGX, LON_PAD))
    field_s[...] = field.reshape(LEV, ROWS_DEV, LON_PAD)
    local[3].wait()
    local[4].wait()

    for n in range(0, LON_DEV, LANES):
        at = slice(n, min(n + LANES, LON_DEV))
        levels = [field_s[v, :, at] for v in range(LEV)]

        @pl.loop(0, POUT)
        def _(p):
            below = bracket_v[p, :, at]
            weight = frac_v[p, :, at]
            low, high = levels, levels[1:] + levels[-1:]
            for bit in range(4):
                mask = ((below >> bit) & 1) == 1
                low = [jnp.where(mask, b, a) for a, b in zip(low[0::2], low[1::2])]
                high = [jnp.where(mask, b, a) for a, b in zip(high[0::2], high[1::2])]
            out_ref[p, :, at] = (1.0 - weight) * low[0] + weight * high[0]

    wait_all(send1.at[pl.ds(0, NZ - 1)], send_sem.at[0])
    wait_all(send2.at[pl.ds(0, NYC - 1)], send_sem.at[1])
    wait_all(send3.at[pl.ds(0, NZ - 1)], send_sem.at[2])
    wait_all(recv4.at[pl.ds(0, NX - 1)], send_sem.at[3])
    wait_all(recv4.at[0, pl.ds(0, NYC - 1)], send_sem.at[3])


def shards(fourier, lat_of_row, wave_order, analysis, synthesis, bracket, frac):
    lat = lat_of_row.reshape(LOOPS_DEV, LANES)
    wave = wave_order.reshape(1, WAVES)
    fourier = jnp.transpose(fourier, (1, 3, 2, 0))
    vmem = pl.BlockSpec(memory_space=pltpu.VMEM)
    hbm = pl.BlockSpec(memory_space=pl.ANY)
    return pl.pallas_call(
        kernel,
        out_shape=jax.ShapeDtypeStruct((POUT, ROWS_DEV, LON_DEV), F32),
        in_specs=[vmem, vmem, hbm, hbm, hbm, hbm, hbm],
        out_specs=vmem,
        scratch_shapes=[
            pltpu.VMEM((2, LOOPS_DEV, LEV_DEV, WAVES), BF16),
            pltpu.VMEM((WAVES, HALF), BF16),
            pltpu.VMEM((NGX * ROWS_DEV, WAVES), BF16),
            pltpu.VMEM((POUT, ROWS_DEV, LON_DEV), I32),
            pltpu.VMEM((POUT, ROWS_DEV, LON_DEV), F32),
            pltpu.VMEM((NZ, 16, LANES), BF16),
            pltpu.VMEM((NZ, 16, LANES), BF16),
            pltpu.VMEM((NYC, NZ, 2 * LANES), BF16),
            pltpu.VMEM((NYC, NZ, 2 * LANES), BF16),
            pltpu.VMEM((NZ, NYC, LANES), BF16),
            pltpu.VMEM((NZ, NYC, LANES), BF16),
            pltpu.VMEM((NYC, NZ, LANES), BF16),
            pltpu.VMEM((NX, NYC, NZ, LANES), BF16),
            pltpu.VMEM((2, 24, LANES), I32),
            pltpu.VMEM((WAVES, NLAT), BF16),
            pltpu.VMEM((NZ * 16, LANES), F32),
            pltpu.VMEM((NGX, LANES), F32),
            pltpu.VMEM((NGX * ROWS_DEV, WAVES), F32),
            pltpu.VMEM((NGX, ROWS_DEV * WAVES), BF16),
            pltpu.VMEM((WAVES, LANES), I32),
            pltpu.VMEM((2, NGX, LON_PAD), BF16),
            pltpu.VMEM((LEV, ROWS_DEV, LON_PAD), F32),
            pltpu.SemaphoreType.DMA((5,)),
            pltpu.SemaphoreType.DMA((4,)),
            pltpu.SemaphoreType.DMA((4,)),
        ],
        compiler_params=pltpu.CompilerParams(
            collective_id=0, has_side_effects=True, vmem_limit_bytes=32 * 1024 * 1024
        ),
        cost_estimate=pl.CostEstimate(flops=10**9, bytes_accessed=1400000, transcendentals=0),
    )(
        lat, wave, fourier, analysis.reshape(WAVES, HALF),
        synthesis.reshape(NGX * ROWS_DEV, WAVES), bracket, frac,
    )


def solution(mesh):
    placed = (
        P(None, None, "grp", "gx"),
        P(),
        P(),
        P("gx", None, None),
        P("gx", None, None),
        P(None, "gx", "grp"),
        P(None, "gx", "grp"),
    )
    return jax.shard_map(
        shards, mesh=mesh, in_specs=placed, out_specs=P(None, "gx", "grp"), check_vma=False
    )
```

```python
import functools
import math

import jax
import jax.numpy as jnp
from jax import lax
from jax.experimental import pallas as pl
from jax.experimental.pallas import tpu as pltpu
from jax.sharding import PartitionSpec as P

MESH = pl.DeviceIdType.MESH
F32, BF16, I32 = jnp.float32, jnp.bfloat16, jnp.int32

NX, NZ, NYC = 4, 16, 8
NGX = NZ * NYC
MTOT, NLAT, NLON = 1280, 2560, 3600
WAVES = 128
FIRST_WAVE = MTOT - WAVES
LEV_DEV, ROWS_DEV, LOOPS_DEV, LON_DEV, POUT, LEV = 4, 8, 20, 900, 8, 16
HALF = NLAT // 2
LANES = 128
LON_PAD = 1024


def iota(shape, axis):
    return lax.broadcasted_iota(I32, shape, axis)


def nt_dot(a, b):
    return lax.dot_general(a, b, (((1,), (1,)), ((), ())), preferred_element_type=F32)


def nn_dot(a, b):
    return lax.dot_general(a, b, (((1,), (0,)), ((), ())), preferred_element_type=F32)


def ordered_waves(fourier, wave):
    pick = (iota((WAVES, WAVES), 0) == wave).astype(F32)
    pick = pick.T.astype(BF16)
    rows = jnp.concatenate([fourier[0].astype(F32), fourier[1].astype(F32)], axis=1)
    rows = rows.reshape(LOOPS_DEV * 8, WAVES)
    rows = jnp.concatenate([rows, jnp.zeros((256 - LOOPS_DEV * 8, WAVES), F32)], axis=0)
    return nt_dot(pick, rows.astype(BF16))


def loop_lats(lat):
    flat = iota((24, LANES), 1) * LOOPS_DEV + jnp.minimum(iota((24, LANES), 0), LOOPS_DEV - 1)
    high, low = flat >> 7, flat & (LANES - 1)
    out = jnp.zeros((24, LANES), I32)
    for a in range(LOOPS_DEV):
        row = jnp.broadcast_to(lat[a : a + 1], (24, LANES))
        out = jnp.where(high == a, jnp.take_along_axis(row, low, axis=1), out)
    return out


def table_tile(wave_col, lon):
    turns = wave_col * lon
    quarter = jnp.floor(turns.astype(F32) * (4.0 / NLON) + 0.5).astype(I32)
    rest = (turns - quarter * (NLON // 4)).astype(F32) * (2.0 * math.pi / NLON)
    sq = rest * rest
    c = 1.0 + sq * (-0.5 + sq * (1.0 / 24 + sq * (-1.0 / 720 + sq * (1.0 / 40320))))
    s = rest * (1.0 + sq * (-1.0 / 6 + sq * (1.0 / 120 + sq * (-1.0 / 5040 + sq * (1.0 / 362880)))))
    odd = (quarter & 1) == 1
    cos = jnp.where(odd, s, c)
    sin = jnp.where(odd, c, s)
    cos = jnp.where(((quarter + 1) & 2) == 2, -2.0 * cos, 2.0 * cos)
    sin = jnp.where((quarter & 2) == 2, 2.0 * sin, -2.0 * sin)
    return cos.astype(BF16), sin.astype(BF16)


def farthest_first(step, half):
    return half + ((step + 1) >> 1) * (1 - 2 * (step & 1))


def kernel(
    fourier_ref, wave_ref, lat_ref, analysis_ref, synthesis_ref, bracket_ref, frac_ref,
    out_ref,
    fourier_v, wave_v, lat_v, analysis_v, synthesis_v, bracket_v, frac_v,
    send1, recv1, send2, recv2, send3, recv3,
    lats_s, sorted_s, spread_s, syn_f, syn_s, wave_s, table_s, field_s,
    local_sem, send_sem, recv_sem,
):
    x = lax.axis_index("grp")
    gx = lax.axis_index("gx")
    z, yc = gx >> 3, gx & (NYC - 1)

    def peers(action):
        def near(tz, count):
            for j in range(count):
                action((tz << 3) + ((yc + farthest_first(j, NYC // 2)) & (NYC - 1)))

        @pl.loop(0, NZ - 1)
        def _(k):
            near((z + farthest_first(k, NZ // 2)) & (NZ - 1), NYC)

        near(z, NYC - 1)

    barrier = pltpu.get_barrier_semaphore()

    def signal(tx, to):
        pl.semaphore_signal(barrier, inc=1, device_id=(tx, to), device_id_type=MESH)

    peers(lambda to: signal(x, to))
    for d in (2, 1, 3):
        signal((x + d) & (NX - 1), gx)

    local = [
        pltpu.make_async_copy(src, dst, local_sem.at[i])
        for i, (src, dst) in enumerate(
            (
                (fourier_ref, fourier_v),
                (wave_ref, wave_v),
                (lat_ref, lat_v),
                (analysis_ref, analysis_v),
                (synthesis_ref, synthesis_v),
                (bracket_ref, bracket_v),
                (frac_ref, frac_v),
            )
        )
    ]
    for copy in local:
        copy.start()

    def exchange(send, recv, stage):
        def one(to):
            pltpu.make_async_remote_copy(
                src_ref=send(to),
                dst_ref=recv(gx),
                send_sem=send_sem.at[stage],
                recv_sem=recv_sem.at[stage],
                device_id=(x, to),
                device_id_type=MESH,
            ).start()

        peers(one)
        pltpu.make_async_copy(send(gx), recv(gx), recv_sem.at[stage]).start()

    def wait_all(ref, sem):
        pltpu.make_async_copy(ref, ref, sem).wait()

    local[0].wait()
    local[1].wait()
    wave = wave_v[...]
    ordered = ordered_waves(fourier_v[...], wave)
    spread_s[pl.ds(0, NGX, stride=2), :] = ordered[:, :LANES]
    spread_s[pl.ds(1, NGX, stride=2), :] = ordered[:, LANES:]
    send1.reshape(2 * NGX, LANES)[...] = spread_s[...].astype(BF16)
    pl.semaphore_wait(barrier, NGX - 1 + NX - 1)
    exchange(lambda to: send1.at[to], lambda to: recv1.at[to], 0)

    local[2].wait()
    lats = loop_lats(lat_v[...])
    own = jnp.sum(jnp.where(iota((1, WAVES), 1) == gx, wave, 0), axis=1, keepdims=True)
    pole = jnp.minimum(lats, NLAT - 1 - lats)
    live = 2 * (FIRST_WAVE + own) < 20 + 4 * pole
    lats_s[0] = jnp.where(live, pole, -1)
    lats_s[1] = jnp.where(lats >= HALF, 1, 0)
    local[3].wait()

    @pl.loop(0, LOOPS_DEV // 2)
    def _(pair):
        row = lats_s[0, pl.ds(2 * pair, 2), :]
        south = lats_s[1, pl.ds(2 * pair, 2), :]
        row = jnp.concatenate([row[0:1], row[1:2]], axis=1)
        south = jnp.concatenate([south[0:1], south[1:2]], axis=1)
        total = jnp.zeros((WAVES, 2 * LANES), F32)
        for j in range(0, HALF, 256):
            hot = (iota((256, 2 * LANES), 0) + j == row).astype(F32).astype(BF16)
            total += nn_dot(analysis_v[:, j : j + 256], hot)
        odd = iota((WAVES, 2 * LANES), 0) & 1
        total = jnp.where((odd * south) == 1, -total, total)
        sorted_s[:, pl.ds(pl.multiple_of(pair * 256, 256), 256)] = total.astype(BF16)

    local[4].wait()
    syn_f[...] = synthesis_v[...].astype(F32)
    for ri in range(ROWS_DEV):
        syn_s[:, ri * LANES : (ri + 1) * LANES] = syn_f[pl.ds(ri, NGX, stride=ROWS_DEV), :].astype(BF16)

    wait_all(recv1, recv_sem.at[0])
    spread_s[...] = recv1.reshape(2 * NGX, LANES)[...].astype(F32)
    head = spread_s[pl.ds(0, NGX, stride=2), :].T
    tail = spread_s[pl.ds(1, NGX, stride=2), :].T
    loops = jnp.concatenate([head, tail], axis=0)
    loops = jnp.concatenate([loops[8 * s : 8 * s + 8] for s in range(LOOPS_DEV)], axis=1)
    spec = nt_dot(loops.astype(BF16), sorted_s[...])
    spec = jnp.where(iota((8, WAVES), 1) < WAVES - own, spec, 0.0).astype(BF16).astype(F32)
    wide = jnp.broadcast_to(spec[:, None, :], (8, ROWS_DEV, WAVES)).reshape(8 * ROWS_DEV, WAVES)
    ri = iota((8 * ROWS_DEV, WAVES), 0) & (ROWS_DEV - 1)
    wide = jnp.concatenate([jnp.where(ri == r, wide, 0.0) for r in range(ROWS_DEV)], axis=1)
    wide = jnp.concatenate([wide, jnp.zeros_like(wide)], axis=0).astype(BF16)
    send2[...] = nt_dot(syn_s[...], wide).astype(BF16).astype(F32)

    exchange(lambda to: send2.at[pl.ds(to, 1)], lambda to: recv2.at[pl.ds(to, 1)], 1)
    wave_s[...] = jnp.broadcast_to(wave.astype(F32), (WAVES, WAVES)).T.astype(I32) + FIRST_WAVE
    lon_start = x * LON_DEV

    @pl.loop(0, NGX // 16)
    def _(i):
        at = pl.ds(pl.multiple_of(i * 16, 16), 16)
        col = wave_s[at, :]
        for n in range(0, LON_PAD, LANES):
            lon = iota((16, LANES), 1) + (lon_start + n)
            cos, sin = table_tile(col, lon)
            table_s[0, at, n : n + LANES] = cos
            table_s[1, at, n : n + LANES] = sin

    local[5].wait()
    local[6].wait()

    wait_all(recv2, recv_sem.at[1])
    send3[...] = recv2[...].T[: 8 * ROWS_DEV].astype(BF16)
    for d in (2, 1, 3):
        pltpu.make_async_remote_copy(
            src_ref=send3,
            dst_ref=recv3.at[x],
            send_sem=send_sem.at[2],
            recv_sem=recv_sem.at[2],
            device_id=((x + d) & (NX - 1), gx),
            device_id_type=MESH,
        ).start()
    pltpu.make_async_copy(send3, recv3.at[x], recv_sem.at[2]).start()

    wait_all(recv3, recv_sem.at[2])
    half = 4 * ROWS_DEV
    rows = jnp.concatenate(
        [jnp.concatenate([recv3[v, :half], recv3[v, half:]], axis=1) for v in range(NX)], axis=0
    )
    field = nn_dot(rows, table_s[...].reshape(2 * NGX, LON_PAD))
    field_s[...] = field.reshape(LEV, ROWS_DEV, LON_PAD)

    for n in range(0, LON_DEV, LANES):
        at = slice(n, min(n + LANES, LON_DEV))
        levels = [field_s[v, :, at] for v in range(LEV)]

        @pl.loop(0, POUT)
        def _(p):
            below = bracket_v[p, :, at]
            weight = frac_v[p, :, at]
            low, high = levels, levels[1:] + levels[-1:]
            for bit in range(4):
                mask = ((below >> bit) & 1) == 1
                low = [jnp.where(mask, b, a) for a, b in zip(low[0::2], low[1::2])]
                high = [jnp.where(mask, b, a) for a, b in zip(high[0::2], high[1::2])]
            out_ref[p, :, at] = (1.0 - weight) * low[0] + weight * high[0]

    wait_all(send1.at[pl.ds(0, NGX - 1)], send_sem.at[0])
    wait_all(send2.at[pl.ds(0, NGX - 1)], send_sem.at[1])
    wait_all(recv3.at[pl.ds(0, NX - 1)], send_sem.at[2])


def shards(fourier, lat_of_row, wave_order, analysis, synthesis, bracket, frac):
    lat = lat_of_row.reshape(LOOPS_DEV, LANES)
    wave = wave_order.reshape(1, WAVES)
    fourier = jnp.transpose(fourier, (1, 3, 2, 0))
    vmem = pl.BlockSpec(memory_space=pltpu.VMEM)
    hbm = pl.BlockSpec(memory_space=pltpu.HBM)
    return pl.pallas_call(
        kernel,
        out_shape=jax.ShapeDtypeStruct((POUT, ROWS_DEV, LON_DEV), F32),
        in_specs=[hbm] * 7,
        out_specs=vmem,
        scratch_shapes=[
            pltpu.VMEM((2, LOOPS_DEV, LEV_DEV, WAVES), BF16),
            pltpu.VMEM((1, WAVES), I32),
            pltpu.VMEM((LOOPS_DEV, LANES), I32),
            pltpu.VMEM((WAVES, HALF), BF16),
            pltpu.VMEM((NGX * ROWS_DEV, WAVES), BF16),
            pltpu.VMEM((POUT, ROWS_DEV, LON_DEV), I32),
            pltpu.VMEM((POUT, ROWS_DEV, LON_DEV), F32),
            pltpu.VMEM((NGX, 2, LANES), BF16),
            pltpu.VMEM((NGX, 2, LANES), BF16),
            pltpu.VMEM((NGX, LANES), F32),
            pltpu.VMEM((NGX, LANES), F32),
            pltpu.VMEM((8 * ROWS_DEV, NGX), BF16),
            pltpu.VMEM((NX, 8 * ROWS_DEV, NGX), BF16),
            pltpu.VMEM((2, 24, LANES), I32),
            pltpu.VMEM((WAVES, NLAT), BF16),
            pltpu.VMEM((2 * NGX, LANES), F32),
            pltpu.VMEM((NGX * ROWS_DEV, WAVES), F32),
            pltpu.VMEM((NGX, ROWS_DEV * WAVES), BF16),
            pltpu.VMEM((WAVES, LANES), I32),
            pltpu.VMEM((2, NGX, LON_PAD), BF16),
            pltpu.VMEM((LEV, ROWS_DEV, LON_PAD), F32),
            pltpu.SemaphoreType.DMA((7,)),
            pltpu.SemaphoreType.DMA((3,)),
            pltpu.SemaphoreType.DMA((3,)),
        ],
        compiler_params=pltpu.CompilerParams(
            collective_id=0, has_side_effects=True, vmem_limit_bytes=56 * 1024 * 1024
        ),
        cost_estimate=pl.CostEstimate(flops=10**9, bytes_accessed=1400000, transcendentals=0),
    )(
        fourier, wave, lat, analysis.reshape(WAVES, HALF),
        synthesis.reshape(NGX * ROWS_DEV, WAVES), bracket, frac,
    )


def solution(mesh):
    placed = (
        P(None, None, "grp", "gx"),
        P(),
        P(),
        P("gx", None, None),
        P("gx", None, None),
        P(None, "gx", "grp"),
        P(None, "gx", "grp"),
    )
    return jax.shard_map(
        shards, mesh=mesh, in_specs=placed, out_specs=P(None, "gx", "grp"), check_vma=False
    )
```

```python
import functools
import math

import jax
import jax.numpy as jnp
from jax import lax
from jax.experimental import pallas as pl
from jax.experimental.pallas import tpu as pltpu
from jax.sharding import PartitionSpec as P

MESH = pl.DeviceIdType.MESH
F32, BF16, I32 = jnp.float32, jnp.bfloat16, jnp.int32

NX, NZ, NYC = 4, 16, 8
NGX = NZ * NYC
MTOT, NLAT, NLON = 1280, 2560, 3600
WAVES = 128
FIRST_WAVE = MTOT - WAVES
LEV_DEV, ROWS_DEV, LOOPS_DEV, LON_DEV, POUT, LEV = 4, 8, 20, 900, 8, 16
HALF = NLAT // 2
LANES = 128
LON_PAD = 1024


def iota(shape, axis):
    return lax.broadcasted_iota(I32, shape, axis)


def nt_dot(a, b):
    return lax.dot_general(a, b, (((1,), (1,)), ((), ())), preferred_element_type=F32)


def nn_dot(a, b):
    return lax.dot_general(a, b, (((1,), (0,)), ((), ())), preferred_element_type=F32)


def ordered_waves(fourier, wave):
    pick = (iota((WAVES, WAVES), 0) == wave).astype(F32)
    pick = pick.T.astype(BF16)
    rows = jnp.concatenate([fourier[0].astype(F32), fourier[1].astype(F32)], axis=1)
    rows = rows.reshape(LOOPS_DEV * 8, WAVES)
    rows = jnp.concatenate([rows, jnp.zeros((256 - LOOPS_DEV * 8, WAVES), F32)], axis=0)
    return nt_dot(pick, rows.astype(BF16))


def loop_lats(lat):
    flat = iota((24, LANES), 1) * LOOPS_DEV + jnp.minimum(iota((24, LANES), 0), LOOPS_DEV - 1)
    high, low = flat >> 7, flat & (LANES - 1)
    out = jnp.zeros((24, LANES), I32)
    for a in range(LOOPS_DEV):
        row = jnp.broadcast_to(lat[a : a + 1], (24, LANES))
        out = jnp.where(high == a, jnp.take_along_axis(row, low, axis=1), out)
    return out


def table_tile(wave_col, lon):
    turns = wave_col * lon
    quarter = jnp.floor(turns.astype(F32) * (4.0 / NLON) + 0.5).astype(I32)
    rest = (turns - quarter * (NLON // 4)).astype(F32) * (2.0 * math.pi / NLON)
    sq = rest * rest
    c = 1.0 + sq * (-0.5 + sq * (1.0 / 24 + sq * (-1.0 / 720 + sq * (1.0 / 40320))))
    s = rest * (1.0 + sq * (-1.0 / 6 + sq * (1.0 / 120 + sq * (-1.0 / 5040 + sq * (1.0 / 362880)))))
    odd = (quarter & 1) == 1
    cos = jnp.where(odd, s, c)
    sin = jnp.where(odd, c, s)
    cos = jnp.where(((quarter + 1) & 2) == 2, -2.0 * cos, 2.0 * cos)
    sin = jnp.where((quarter & 2) == 2, 2.0 * sin, -2.0 * sin)
    return cos.astype(BF16), sin.astype(BF16)


def farthest_first(step, half):
    return half + ((step + 1) >> 1) * (1 - 2 * (step & 1))


def kernel(
    fourier_ref, wave_ref, lat_ref, analysis_ref, synthesis_ref, bracket_ref, frac_ref,
    out_ref,
    fourier_v, wave_v, lat_v, analysis_v, synthesis_v, bracket_v, frac_v,
    send1, recv1, send2, recv2, send3, recv3,
    lats_s, sorted_s, spread_s, syn_f, syn_s, wave_s, table_s, field_s,
    local_sem, send_sem, recv_sem,
):
    x = lax.axis_index("grp")
    gx = lax.axis_index("gx")
    z, yc = gx >> 3, gx & (NYC - 1)

    def peers(action):
        def near(tz, count):
            for j in range(count):
                action((tz << 3) + ((yc + farthest_first(j, NYC // 2)) & (NYC - 1)))

        @pl.loop(0, NZ - 1)
        def _(k):
            near((z + farthest_first(k, NZ // 2)) & (NZ - 1), NYC)

        near(z, NYC - 1)

    barrier = pltpu.get_barrier_semaphore()

    def signal(tx, to):
        pl.semaphore_signal(barrier, inc=1, device_id=(tx, to), device_id_type=MESH)

    peers(lambda to: signal(x, to))
    for d in (2, 1, 3):
        signal((x + d) & (NX - 1), gx)

    local = [
        pltpu.make_async_copy(src, dst, local_sem.at[i])
        for i, (src, dst) in enumerate(
            (
                (fourier_ref, fourier_v),
                (wave_ref, wave_v),
                (lat_ref, lat_v),
                (analysis_ref, analysis_v),
                (synthesis_ref, synthesis_v),
                (bracket_ref, bracket_v),
                (frac_ref, frac_v),
            )
        )
    ]
    for copy in local:
        copy.start()

    def exchange(send, recv, stage):
        def one(to):
            pltpu.make_async_remote_copy(
                src_ref=send(to),
                dst_ref=recv(gx),
                send_sem=send_sem.at[stage],
                recv_sem=recv_sem.at[stage],
                device_id=(x, to),
                device_id_type=MESH,
            ).start()

        peers(one)
        pltpu.make_async_copy(send(gx), recv(gx), recv_sem.at[stage]).start()

    def wait_all(ref, sem):
        pltpu.make_async_copy(ref, ref, sem).wait()

    local[0].wait()
    local[1].wait()
    wave = wave_v[...]
    ordered = ordered_waves(fourier_v[...], wave)
    spread_s[pl.ds(0, NGX, stride=2), :] = ordered[:, :LANES]
    spread_s[pl.ds(1, NGX, stride=2), :] = ordered[:, LANES:]
    send1.reshape(2 * NGX, LANES)[...] = spread_s[...].astype(BF16)
    pl.semaphore_wait(barrier, NGX - 1 + NX - 1)
    exchange(lambda to: send1.at[to], lambda to: recv1.at[to], 0)

    local[2].wait()
    lats = loop_lats(lat_v[...])
    own = jnp.sum(jnp.where(iota((1, WAVES), 1) == gx, wave, 0), axis=1, keepdims=True)
    pole = jnp.minimum(lats, NLAT - 1 - lats)
    live = 2 * (FIRST_WAVE + own) < 20 + 4 * pole
    lats_s[0] = jnp.where(live, pole, -1)
    lats_s[1] = jnp.where(lats >= HALF, 1, 0)
    local[3].wait()

    @pl.loop(0, LOOPS_DEV // 2)
    def _(pair):
        row = lats_s[0, pl.ds(2 * pair, 2), :]
        south = lats_s[1, pl.ds(2 * pair, 2), :]
        row = jnp.concatenate([row[0:1], row[1:2]], axis=1)
        south = jnp.concatenate([south[0:1], south[1:2]], axis=1)
        total = jnp.zeros((WAVES, 2 * LANES), F32)
        for j in range(0, HALF, 256):
            hot = (iota((256, 2 * LANES), 0) + j == row).astype(F32).astype(BF16)
            total += nn_dot(analysis_v[:, j : j + 256], hot)
        odd = iota((WAVES, 2 * LANES), 0) & 1
        total = jnp.where((odd * south) == 1, -total, total)
        sorted_s[:, pl.ds(pl.multiple_of(pair * 256, 256), 256)] = total.astype(BF16)

    local[4].wait()
    syn_f[...] = synthesis_v[...].astype(F32)
    for ri in range(ROWS_DEV):
        syn_s[:, ri * LANES : (ri + 1) * LANES] = syn_f[pl.ds(ri, NGX, stride=ROWS_DEV), :].astype(BF16)

    wait_all(recv1, recv_sem.at[0])
    spread_s[...] = recv1.reshape(2 * NGX, LANES)[...].astype(F32)
    head = spread_s[pl.ds(0, NGX, stride=2), :].T
    tail = spread_s[pl.ds(1, NGX, stride=2), :].T
    loops = jnp.concatenate([head, tail], axis=0)
    loops = jnp.concatenate([loops[8 * s : 8 * s + 8] for s in range(LOOPS_DEV)], axis=1)
    spec = nt_dot(loops.astype(BF16), sorted_s[...])
    spec = jnp.where(iota((8, WAVES), 1) < WAVES - own, spec, 0.0).astype(BF16).astype(F32)
    wide = jnp.broadcast_to(spec[:, None, :], (8, ROWS_DEV, WAVES)).reshape(8 * ROWS_DEV, WAVES)
    ri = iota((8 * ROWS_DEV, WAVES), 0) & (ROWS_DEV - 1)
    wide = jnp.concatenate([jnp.where(ri == r, wide, 0.0) for r in range(ROWS_DEV)], axis=1)
    wide = jnp.concatenate([wide, jnp.zeros_like(wide)], axis=0).astype(BF16)
    send2[...] = nt_dot(syn_s[...], wide).astype(BF16).astype(F32)

    exchange(lambda to: send2.at[pl.ds(to, 1)], lambda to: recv2.at[pl.ds(to, 1)], 1)
    wave_s[...] = jnp.broadcast_to(wave.astype(F32), (WAVES, WAVES)).T.astype(I32) + FIRST_WAVE
    lon_start = x * LON_DEV

    @pl.loop(0, NGX // 16)
    def _(i):
        at = pl.ds(pl.multiple_of(i * 16, 16), 16)
        col = wave_s[at, :]
        for n in range(0, LON_PAD, LANES):
            lon = iota((16, LANES), 1) + (lon_start + n)
            cos, sin = table_tile(col, lon)
            table_s[0, at, n : n + LANES] = cos
            table_s[1, at, n : n + LANES] = sin

    local[5].wait()
    local[6].wait()

    wait_all(recv2, recv_sem.at[1])
    send3[...] = recv2[...].T[: 8 * ROWS_DEV].astype(BF16)
    for d in (2, 1, 3):
        pltpu.make_async_remote_copy(
            src_ref=send3,
            dst_ref=recv3.at[x],
            send_sem=send_sem.at[2],
            recv_sem=recv_sem.at[2],
            device_id=((x + d) & (NX - 1), gx),
            device_id_type=MESH,
        ).start()
    pltpu.make_async_copy(send3, recv3.at[x], recv_sem.at[2]).start()

    wait_all(recv3, recv_sem.at[2])
    half = 4 * ROWS_DEV
    rows = jnp.concatenate(
        [jnp.concatenate([recv3[v, :half], recv3[v, half:]], axis=1) for v in range(NX)], axis=0
    )
    field = nn_dot(rows, table_s[...].reshape(2 * NGX, LON_PAD))
    field_s[...] = field.reshape(LEV, ROWS_DEV, LON_PAD)

    for n in range(0, LON_DEV, LANES):
        at = slice(n, min(n + LANES, LON_DEV))
        levels = [field_s[v, :, at] for v in range(LEV)]

        @pl.loop(0, POUT)
        def _(p):
            below = bracket_v[p, :, at]
            weight = frac_v[p, :, at]
            low, high = levels, levels[1:] + levels[-1:]
            for bit in range(4):
                mask = ((below >> bit) & 1) == 1
                low = [jnp.where(mask, b, a) for a, b in zip(low[0::2], low[1::2])]
                high = [jnp.where(mask, b, a) for a, b in zip(high[0::2], high[1::2])]
            out_ref[p, :, at] = (1.0 - weight) * low[0] + weight * high[0]

    wait_all(send1.at[pl.ds(0, NGX - 1)], send_sem.at[0])
    wait_all(send2.at[pl.ds(0, NGX - 1)], send_sem.at[1])
    wait_all(recv3.at[pl.ds(0, NX - 1)], send_sem.at[2])


def shards(fourier, lat_of_row, wave_order, analysis, synthesis, bracket, frac):
    lat = lat_of_row.reshape(LOOPS_DEV, LANES)
    wave = wave_order.reshape(1, WAVES)
    fourier = jnp.transpose(fourier, (1, 3, 2, 0))
    vmem = pl.BlockSpec(memory_space=pltpu.VMEM)
    hbm = pl.BlockSpec(memory_space=pltpu.HBM)
    return pl.pallas_call(
        kernel,
        out_shape=pltpu.VMEM((POUT, ROWS_DEV, LON_DEV), F32),
        in_specs=[hbm] * 7,
        out_specs=vmem,
        scratch_shapes=[
            pltpu.VMEM((2, LOOPS_DEV, LEV_DEV, WAVES), BF16),
            pltpu.VMEM((1, WAVES), I32),
            pltpu.VMEM((LOOPS_DEV, LANES), I32),
            pltpu.VMEM((WAVES, HALF), BF16),
            pltpu.VMEM((NGX * ROWS_DEV, WAVES), BF16),
            pltpu.VMEM((POUT, ROWS_DEV, LON_DEV), I32),
            pltpu.VMEM((POUT, ROWS_DEV, LON_DEV), F32),
            pltpu.VMEM((NGX, 2, LANES), BF16),
            pltpu.VMEM((NGX, 2, LANES), BF16),
            pltpu.VMEM((NGX, LANES), F32),
            pltpu.VMEM((NGX, LANES), F32),
            pltpu.VMEM((8 * ROWS_DEV, NGX), BF16),
            pltpu.VMEM((NX, 8 * ROWS_DEV, NGX), BF16),
            pltpu.VMEM((2, 24, LANES), I32),
            pltpu.VMEM((WAVES, NLAT), BF16),
            pltpu.VMEM((2 * NGX, LANES), F32),
            pltpu.VMEM((NGX * ROWS_DEV, WAVES), F32),
            pltpu.VMEM((NGX, ROWS_DEV * WAVES), BF16),
            pltpu.VMEM((WAVES, LANES), I32),
            pltpu.VMEM((2, NGX, LON_PAD), BF16),
            pltpu.VMEM((LEV, ROWS_DEV, LON_PAD), F32),
            pltpu.SemaphoreType.DMA((7,)),
            pltpu.SemaphoreType.DMA((3,)),
            pltpu.SemaphoreType.DMA((3,)),
        ],
        compiler_params=pltpu.CompilerParams(
            collective_id=0, has_side_effects=True, vmem_limit_bytes=56 * 1024 * 1024
        ),
        cost_estimate=pl.CostEstimate(flops=10**9, bytes_accessed=1400000, transcendentals=0),
    )(
        fourier, wave, lat, analysis.reshape(WAVES, HALF),
        synthesis.reshape(NGX * ROWS_DEV, WAVES), bracket, frac,
    )


def solution(mesh):
    placed = (
        P(None, None, "grp", "gx"),
        P(),
        P(),
        P("gx", None, None),
        P("gx", None, None),
        P(None, "gx", "grp"),
        P(None, "gx", "grp"),
    )
    return jax.shard_map(
        shards, mesh=mesh, in_specs=placed, out_specs=P(None, "gx", "grp"), check_vma=False
    )
```

```python
import functools
import math

import jax
import jax.numpy as jnp
from jax import lax
from jax.experimental import pallas as pl
from jax.experimental.pallas import tpu as pltpu
from jax.sharding import PartitionSpec as P

MESH = pl.DeviceIdType.MESH
F32, BF16, I32 = jnp.float32, jnp.bfloat16, jnp.int32

NX, NZ, NYC = 4, 16, 8
NGX = NZ * NYC
MTOT, NLAT, NLON = 1280, 2560, 3600
WAVES = 128
FIRST_WAVE = MTOT - WAVES
LEV_DEV, ROWS_DEV, LOOPS_DEV, LON_DEV, POUT, LEV = 4, 8, 20, 900, 8, 16
HALF = NLAT // 2
LANES = 128
LON_PAD = 1024


def iota(shape, axis):
    return lax.broadcasted_iota(I32, shape, axis)


def nt_dot(a, b):
    return lax.dot_general(a, b, (((1,), (1,)), ((), ())), preferred_element_type=F32)


def nn_dot(a, b):
    return lax.dot_general(a, b, (((1,), (0,)), ((), ())), preferred_element_type=F32)


def ordered_waves(fourier, wave):
    pick = (iota((WAVES, WAVES), 0) == wave).astype(F32)
    pick = pick.T.astype(BF16)
    rows = jnp.concatenate([fourier[0].astype(F32), fourier[1].astype(F32)], axis=1)
    rows = rows.reshape(LOOPS_DEV * 8, WAVES)
    rows = jnp.concatenate([rows, jnp.zeros((256 - LOOPS_DEV * 8, WAVES), F32)], axis=0)
    return nt_dot(pick, rows.astype(BF16))


def loop_lats(lat):
    flat = iota((24, LANES), 1) * LOOPS_DEV + jnp.minimum(iota((24, LANES), 0), LOOPS_DEV - 1)
    high, low = flat >> 7, flat & (LANES - 1)
    out = jnp.zeros((24, LANES), I32)
    for a in range(LOOPS_DEV):
        row = jnp.broadcast_to(lat[a : a + 1], (24, LANES))
        out = jnp.where(high == a, jnp.take_along_axis(row, low, axis=1), out)
    return out


def table_tile(wave_col, lon):
    turns = wave_col * lon
    quarter = jnp.floor(turns.astype(F32) * (4.0 / NLON) + 0.5).astype(I32)
    rest = (turns - quarter * (NLON // 4)).astype(F32) * (2.0 * math.pi / NLON)
    sq = rest * rest
    c = 1.0 + sq * (-0.5 + sq * (1.0 / 24 + sq * (-1.0 / 720 + sq * (1.0 / 40320))))
    s = rest * (1.0 + sq * (-1.0 / 6 + sq * (1.0 / 120 + sq * (-1.0 / 5040 + sq * (1.0 / 362880)))))
    odd = (quarter & 1) == 1
    cos = jnp.where(odd, s, c)
    sin = jnp.where(odd, c, s)
    cos = jnp.where(((quarter + 1) & 2) == 2, -2.0 * cos, 2.0 * cos)
    sin = jnp.where((quarter & 2) == 2, 2.0 * sin, -2.0 * sin)
    return cos.astype(BF16), sin.astype(BF16)


def one_level(levels, bits):
    for bit in bits:
        levels = [jnp.where(bit, b, a) for a, b in zip(levels[0::2], levels[1::2])]
    return levels[0]


def two_levels(levels, below):
    bits = [(below & (1 << i)) != 0 for i in range(4)]

    def pair(values, bits):
        if not bits:
            return values[0], values[1]
        even, after = pair(values[0::2], bits[1:])
        odd = one_level(values[1::2], bits[1:])
        return jnp.where(bits[0], odd, even), jnp.where(bits[0], after, odd)

    return pair(levels + levels[-1:], bits)


def farthest_first(step, half):
    return half + ((step + 1) >> 1) * (1 - 2 * (step & 1))


def kernel(
    fourier_ref, wave_ref, lat_ref, analysis_ref, synthesis_ref, bracket_ref, frac_ref,
    out_ref,
    fourier_v, wave_v, lat_v, analysis_v, synthesis_v, bracket_v, frac_v,
    send1, recv1, send2, recv2, send3, recv3,
    lats_s, sorted_s, spread_s, syn_f, syn_s, wave_s, table_s, field_s,
    local_sem, send_sem, recv_sem,
):
    x = lax.axis_index("grp")
    gx = lax.axis_index("gx")
    z, yc = gx >> 3, gx & (NYC - 1)

    def peers(action):
        def near(tz, count):
            for j in range(count):
                action((tz << 3) + ((yc + farthest_first(j, NYC // 2)) & (NYC - 1)))

        @pl.loop(0, NZ - 1)
        def _(k):
            near((z + farthest_first(k, NZ // 2)) & (NZ - 1), NYC)

        near(z, NYC - 1)

    barrier = pltpu.get_barrier_semaphore()

    def signal(tx, to):
        pl.semaphore_signal(barrier, inc=1, device_id=(tx, to), device_id_type=MESH)

    peers(lambda to: signal(x, to))
    for d in (2, 1, 3):
        signal((x + d) & (NX - 1), gx)

    local = [
        pltpu.make_async_copy(src, dst, local_sem.at[i])
        for i, (src, dst) in enumerate(
            (
                (fourier_ref, fourier_v),
                (wave_ref, wave_v),
                (lat_ref, lat_v),
                (analysis_ref, analysis_v),
                (synthesis_ref, synthesis_v),
                (bracket_ref, bracket_v),
                (frac_ref, frac_v),
            )
        )
    ]
    for copy in local:
        copy.start()

    def exchange(send, recv, stage):
        def one(to):
            pltpu.make_async_remote_copy(
                src_ref=send(to),
                dst_ref=recv(gx),
                send_sem=send_sem.at[stage],
                recv_sem=recv_sem.at[stage],
                device_id=(x, to),
                device_id_type=MESH,
            ).start()

        peers(one)
        pltpu.make_async_copy(send(gx), recv(gx), recv_sem.at[stage]).start()

    def wait_all(ref, sem):
        pltpu.make_async_copy(ref, ref, sem).wait()

    local[0].wait()
    local[1].wait()
    wave = wave_v[...]
    ordered = ordered_waves(fourier_v[...], wave)
    spread_s[pl.ds(0, NGX, stride=2), :] = ordered[:, :LANES]
    spread_s[pl.ds(1, NGX, stride=2), :] = ordered[:, LANES:]
    send1.reshape(2 * NGX, LANES)[...] = spread_s[...].astype(BF16)
    pl.semaphore_wait(barrier, NGX - 1 + NX - 1)
    exchange(lambda to: send1.at[to], lambda to: recv1.at[to], 0)

    local[2].wait()
    lats = loop_lats(lat_v[...])
    own = jnp.sum(jnp.where(iota((1, WAVES), 1) == gx, wave, 0), axis=1, keepdims=True)
    pole = jnp.minimum(lats, NLAT - 1 - lats)
    live = 2 * (FIRST_WAVE + own) < 20 + 4 * pole
    lats_s[0] = jnp.where(live, pole, -1)
    lats_s[1] = jnp.where(lats >= HALF, 1, 0)
    local[3].wait()

    @pl.loop(0, LOOPS_DEV // 2)
    def _(pair):
        row = lats_s[0, pl.ds(2 * pair, 2), :]
        south = lats_s[1, pl.ds(2 * pair, 2), :]
        row = jnp.concatenate([row[0:1], row[1:2]], axis=1)
        south = jnp.concatenate([south[0:1], south[1:2]], axis=1)
        total = jnp.zeros((WAVES, 2 * LANES), F32)
        for j in range(0, HALF, 256):
            hot = (iota((256, 2 * LANES), 0) + j == row).astype(F32).astype(BF16)
            total += nn_dot(analysis_v[:, j : j + 256], hot)
        odd = iota((WAVES, 2 * LANES), 0) & 1
        total = jnp.where((odd * south) == 1, -total, total)
        sorted_s[:, pl.ds(pl.multiple_of(pair * 256, 256), 256)] = total.astype(BF16)

    local[4].wait()
    syn_f[...] = synthesis_v[...].astype(F32)
    for ri in range(ROWS_DEV):
        syn_s[:, ri * LANES : (ri + 1) * LANES] = syn_f[pl.ds(ri, NGX, stride=ROWS_DEV), :].astype(BF16)

    wait_all(recv1, recv_sem.at[0])
    spread_s[...] = recv1.reshape(2 * NGX, LANES)[...].astype(F32)
    head = spread_s[pl.ds(0, NGX, stride=2), :].T
    tail = spread_s[pl.ds(1, NGX, stride=2), :].T
    loops = jnp.concatenate([head, tail], axis=0)
    loops = jnp.concatenate([loops[8 * s : 8 * s + 8] for s in range(LOOPS_DEV)], axis=1)
    spec = nt_dot(loops.astype(BF16), sorted_s[...])
    spec = jnp.where(iota((8, WAVES), 1) < WAVES - own, spec, 0.0).astype(BF16).astype(F32)
    wide = jnp.broadcast_to(spec[:, None, :], (8, ROWS_DEV, WAVES)).reshape(8 * ROWS_DEV, WAVES)
    ri = iota((8 * ROWS_DEV, WAVES), 0) & (ROWS_DEV - 1)
    wide = jnp.concatenate([jnp.where(ri == r, wide, 0.0) for r in range(ROWS_DEV)], axis=1)
    wide = jnp.concatenate([wide, jnp.zeros_like(wide)], axis=0).astype(BF16)
    send2[...] = nt_dot(syn_s[...], wide).astype(BF16).astype(F32)

    exchange(lambda to: send2.at[pl.ds(to, 1)], lambda to: recv2.at[pl.ds(to, 1)], 1)
    wave_s[...] = jnp.broadcast_to(wave.astype(F32), (WAVES, WAVES)).T.astype(I32) + FIRST_WAVE
    lon_start = x * LON_DEV

    @pl.loop(0, NGX // 16)
    def _(i):
        at = pl.ds(pl.multiple_of(i * 16, 16), 16)
        col = wave_s[at, :]
        for n in range(0, LON_PAD, LANES):
            lon = iota((16, LANES), 1) + (lon_start + n)
            cos, sin = table_tile(col, lon)
            table_s[0, at, n : n + LANES] = cos
            table_s[1, at, n : n + LANES] = sin

    local[5].wait()
    local[6].wait()

    wait_all(recv2, recv_sem.at[1])
    send3[...] = recv2[...].T[: 8 * ROWS_DEV].astype(BF16)
    for d in (2, 1, 3):
        pltpu.make_async_remote_copy(
            src_ref=send3,
            dst_ref=recv3.at[x],
            send_sem=send_sem.at[2],
            recv_sem=recv_sem.at[2],
            device_id=((x + d) & (NX - 1), gx),
            device_id_type=MESH,
        ).start()
    pltpu.make_async_copy(send3, recv3.at[x], recv_sem.at[2]).start()

    wait_all(recv3, recv_sem.at[2])
    half = 4 * ROWS_DEV
    rows = jnp.concatenate(
        [jnp.concatenate([recv3[v, :half], recv3[v, half:]], axis=1) for v in range(NX)], axis=0
    )
    for n in range(0, LON_DEV, 2 * LANES):
        table = table_s[:, :, n : n + 2 * LANES].reshape(2 * NGX, 2 * LANES)
        field = nn_dot(rows, table).reshape(LEV, ROWS_DEV, 2 * LANES)
        for k in range(n, min(n + 2 * LANES, LON_DEV), LANES):
            width = min(LANES, LON_DEV - k)
            levels = [field[v, :, k - n : k - n + width] for v in range(LEV)]
            for p in range(POUT):
                below = bracket_v[p, :, k : k + width]
                weight = frac_v[p, :, k : k + width]
                low, high = two_levels(levels, below)
                out_ref[p, :, k : k + width] = (1.0 - weight) * low + weight * high

    wait_all(send1.at[pl.ds(0, NGX - 1)], send_sem.at[0])
    wait_all(send2.at[pl.ds(0, NGX - 1)], send_sem.at[1])
    wait_all(recv3.at[pl.ds(0, NX - 1)], send_sem.at[2])


def shards(fourier, lat_of_row, wave_order, analysis, synthesis, bracket, frac):
    lat = lat_of_row.reshape(LOOPS_DEV, LANES)
    wave = wave_order.reshape(1, WAVES)
    fourier = jnp.transpose(fourier, (1, 3, 2, 0))
    vmem = pl.BlockSpec(memory_space=pltpu.VMEM)
    hbm = pl.BlockSpec(memory_space=pltpu.HBM)
    return pl.pallas_call(
        kernel,
        out_shape=pltpu.VMEM((POUT, ROWS_DEV, LON_DEV), F32),
        in_specs=[hbm] * 7,
        out_specs=vmem,
        scratch_shapes=[
            pltpu.VMEM((2, LOOPS_DEV, LEV_DEV, WAVES), BF16),
            pltpu.VMEM((1, WAVES), I32),
            pltpu.VMEM((LOOPS_DEV, LANES), I32),
            pltpu.VMEM((WAVES, HALF), BF16),
            pltpu.VMEM((NGX * ROWS_DEV, WAVES), BF16),
            pltpu.VMEM((POUT, ROWS_DEV, LON_DEV), I32),
            pltpu.VMEM((POUT, ROWS_DEV, LON_DEV), F32),
            pltpu.VMEM((NGX, 2, LANES), BF16),
            pltpu.VMEM((NGX, 2, LANES), BF16),
            pltpu.VMEM((NGX, LANES), F32),
            pltpu.VMEM((NGX, LANES), F32),
            pltpu.VMEM((8 * ROWS_DEV, NGX), BF16),
            pltpu.VMEM((NX, 8 * ROWS_DEV, NGX), BF16),
            pltpu.VMEM((2, 24, LANES), I32),
            pltpu.VMEM((WAVES, NLAT), BF16),
            pltpu.VMEM((2 * NGX, LANES), F32),
            pltpu.VMEM((NGX * ROWS_DEV, WAVES), F32),
            pltpu.VMEM((NGX, ROWS_DEV * WAVES), BF16),
            pltpu.VMEM((WAVES, LANES), I32),
            pltpu.VMEM((2, NGX, LON_PAD), BF16),
            pltpu.VMEM((LEV, ROWS_DEV, LON_PAD), F32),
            pltpu.SemaphoreType.DMA((7,)),
            pltpu.SemaphoreType.DMA((3,)),
            pltpu.SemaphoreType.DMA((3,)),
        ],
        compiler_params=pltpu.CompilerParams(
            collective_id=0, has_side_effects=True, vmem_limit_bytes=56 * 1024 * 1024
        ),
        cost_estimate=pl.CostEstimate(flops=10**9, bytes_accessed=1400000, transcendentals=0),
    )(
        fourier, wave, lat, analysis.reshape(WAVES, HALF),
        synthesis.reshape(NGX * ROWS_DEV, WAVES), bracket, frac,
    )


def solution(mesh):
    placed = (
        P(None, None, "grp", "gx"),
        P(),
        P(),
        P("gx", None, None),
        P("gx", None, None),
        P(None, "gx", "grp"),
        P(None, "gx", "grp"),
    )
    return jax.shard_map(
        shards, mesh=mesh, in_specs=placed, out_specs=P(None, "gx", "grp"), check_vma=False
    )
```

```python
import functools
import math

import jax
import jax.numpy as jnp
from jax import lax
from jax.experimental import pallas as pl
from jax.experimental.pallas import tpu as pltpu
from jax.sharding import PartitionSpec as P

MESH = pl.DeviceIdType.MESH
F32, BF16, I32 = jnp.float32, jnp.bfloat16, jnp.int32

NX, NZ, NYC = 4, 16, 8
NGX = NZ * NYC
MTOT, NLAT, NLON = 1280, 2560, 3600
WAVES = 128
FIRST_WAVE = MTOT - WAVES
LEV_DEV, ROWS_DEV, LOOPS_DEV, LON_DEV, POUT, LEV = 4, 8, 20, 900, 8, 16
HALF = NLAT // 2
LANES = 128
LON_PAD = 1024
EARLY = 1
FAR = 3


def iota(shape, axis):
    return lax.broadcasted_iota(I32, shape, axis)


def nt_dot(a, b):
    return lax.dot_general(a, b, (((1,), (1,)), ((), ())), preferred_element_type=F32)


def nn_dot(a, b):
    return lax.dot_general(a, b, (((1,), (0,)), ((), ())), preferred_element_type=F32)


def ordered_waves(fourier, wave):
    pick = (iota((WAVES, WAVES), 0) == wave).astype(F32)
    pick = pick.T.astype(BF16)
    rows = jnp.concatenate([fourier[0].astype(F32), fourier[1].astype(F32)], axis=1)
    rows = rows.reshape(LOOPS_DEV * 8, WAVES)
    rows = jnp.concatenate([rows, jnp.zeros((256 - LOOPS_DEV * 8, WAVES), F32)], axis=0)
    return nt_dot(pick, rows.astype(BF16))


def loop_lats(lat):
    flat = iota((24, LANES), 1) * LOOPS_DEV + jnp.minimum(iota((24, LANES), 0), LOOPS_DEV - 1)
    high, low = flat >> 7, flat & (LANES - 1)
    out = jnp.zeros((24, LANES), I32)
    for a in range(LOOPS_DEV):
        row = jnp.broadcast_to(lat[a : a + 1], (24, LANES))
        out = jnp.where(high == a, jnp.take_along_axis(row, low, axis=1), out)
    return out


def table_tile(wave_col, lon):
    turns = wave_col * lon
    quarter = jnp.floor(turns.astype(F32) * (4.0 / NLON) + 0.5).astype(I32)
    rest = (turns - quarter * (NLON // 4)).astype(F32) * (2.0 * math.pi / NLON)
    sq = rest * rest
    c = 1.0 + sq * (-0.5 + sq * (1.0 / 24 + sq * (-1.0 / 720 + sq * (1.0 / 40320))))
    s = rest * (1.0 + sq * (-1.0 / 6 + sq * (1.0 / 120 + sq * (-1.0 / 5040 + sq * (1.0 / 362880)))))
    odd = (quarter & 1) == 1
    cos = jnp.where(odd, s, c)
    sin = jnp.where(odd, c, s)
    cos = jnp.where(((quarter + 1) & 2) == 2, -2.0 * cos, 2.0 * cos)
    sin = jnp.where((quarter & 2) == 2, 2.0 * sin, -2.0 * sin)
    return cos.astype(BF16), sin.astype(BF16)


def one_level(levels, bits):
    for bit in bits:
        levels = [jnp.where(bit, b, a) for a, b in zip(levels[0::2], levels[1::2])]
    return levels[0]


def two_levels(levels, below):
    bits = [(below & (1 << i)) != 0 for i in range(4)]

    def pair(values, bits):
        if not bits:
            return values[0], values[1]
        even, after = pair(values[0::2], bits[1:])
        odd = one_level(values[1::2], bits[1:])
        return jnp.where(bits[0], odd, even), jnp.where(bits[0], after, odd)

    return pair(levels + levels[-1:], bits)


def farthest_first(step, half):
    return half + ((step + 1) >> 1) * (1 - 2 * (step & 1))


def kernel(
    fourier_ref, wave_ref, lat_ref, analysis_ref, synthesis_ref, bracket_ref, frac_ref,
    out_ref,
    fourier_v, wave_v, lat_v, analysis_v, synthesis_v, bracket_v, frac_v,
    send1, recv1, send2, recv2, send3, recv3, far2, rows_s,
    lats_s, sorted_s, spread_s, syn_f, syn_s, wave_s, table_s, field_s,
    local_sem, send_sem, recv_sem,
):
    x = lax.axis_index("grp")
    gx = lax.axis_index("gx")
    z, yc = gx >> 3, gx & (NYC - 1)

    def near(tz, count, action):
        for j in range(count):
            action((tz << 3) + ((yc + farthest_first(j, NYC // 2)) & (NYC - 1)))

    def peers(action):
        @pl.loop(0, NZ - 1)
        def _(k):
            near((z + farthest_first(k, NZ // 2)) & (NZ - 1), NYC, action)

        near(z, NYC - 1, action)

    early = z < EARLY

    @pl.when(early)
    def _():
        recv2[...] = jnp.zeros((NGX, LANES), F32)
        far2[...] = jnp.zeros((NX, NGX, LANES), F32)

    barrier = pltpu.get_barrier_semaphore()

    def signal(tx, to):
        pl.semaphore_signal(barrier, inc=1, device_id=(tx, to), device_id_type=MESH)

    peers(lambda to: signal(x, to))
    for d in (2, 1, 3):
        signal((x + d) & (NX - 1), gx)

    local = [
        pltpu.make_async_copy(src, dst, local_sem.at[i])
        for i, (src, dst) in enumerate(
            (
                (fourier_ref, fourier_v),
                (wave_ref, wave_v),
                (lat_ref, lat_v),
                (analysis_ref, analysis_v),
                (synthesis_ref, synthesis_v),
                (bracket_ref, bracket_v),
                (frac_ref, frac_v),
            )
        )
    ]
    for copy in local:
        copy.start()

    def push(src, dst, stage, tx, to):
        pltpu.make_async_remote_copy(
            src_ref=src,
            dst_ref=dst,
            send_sem=send_sem.at[stage],
            recv_sem=recv_sem.at[stage],
            device_id=(tx, to),
            device_id_type=MESH,
        ).start()

    def wait_all(ref, sem):
        pltpu.make_async_copy(ref, ref, sem).wait()

    local[0].wait()
    local[1].wait()
    wave = wave_v[...]
    ordered = ordered_waves(fourier_v[...], wave)
    spread_s[pl.ds(0, NGX, stride=2), :] = ordered[:, :LANES]
    spread_s[pl.ds(1, NGX, stride=2), :] = ordered[:, LANES:]
    send1.reshape(2 * NGX, LANES)[...] = spread_s[...].astype(BF16)
    pl.semaphore_wait(barrier, NGX - 1 + NX - 1)
    peers(lambda to: push(send1.at[to], recv1.at[gx], 0, x, to))
    pltpu.make_async_copy(send1.at[gx], recv1.at[gx], recv_sem.at[0]).start()

    local[2].wait()
    lats = loop_lats(lat_v[...])
    own = jnp.sum(jnp.where(iota((1, WAVES), 1) == gx, wave, 0), axis=1, keepdims=True)
    pole = jnp.minimum(lats, NLAT - 1 - lats)
    live = 2 * (FIRST_WAVE + own) < 20 + 4 * pole
    lats_s[0] = jnp.where(live, pole, -1)
    lats_s[1] = jnp.where(lats >= HALF, 1, 0)
    local[3].wait()

    @pl.loop(0, LOOPS_DEV // 2)
    def _(pair):
        row = lats_s[0, pl.ds(2 * pair, 2), :]
        south = lats_s[1, pl.ds(2 * pair, 2), :]
        row = jnp.concatenate([row[0:1], row[1:2]], axis=1)
        south = jnp.concatenate([south[0:1], south[1:2]], axis=1)
        total = jnp.zeros((WAVES, 2 * LANES), F32)
        for j in range(0, HALF, 256):
            hot = (iota((256, 2 * LANES), 0) + j == row).astype(F32).astype(BF16)
            total += nn_dot(analysis_v[:, j : j + 256], hot)
        odd = iota((WAVES, 2 * LANES), 0) & 1
        total = jnp.where((odd * south) == 1, -total, total)
        sorted_s[pl.ds(pl.multiple_of(pair * 256, 256), 256), :] = total.T.astype(BF16)

    local[4].wait()
    syn_f[...] = synthesis_v[...].astype(F32)
    for ri in range(ROWS_DEV):
        syn_s[:, ri * LANES : (ri + 1) * LANES] = syn_f[pl.ds(ri, NGX, stride=ROWS_DEV), :].astype(BF16)

    wait_all(recv1, recv_sem.at[0])
    spread_s[...] = recv1.reshape(2 * NGX, LANES)[...].astype(F32)
    head = spread_s[pl.ds(0, NGX, stride=2), :].T
    tail = spread_s[pl.ds(1, NGX, stride=2), :].T
    loops = jnp.concatenate([head, tail], axis=0)
    loops = jnp.concatenate([loops[8 * s : 8 * s + 8] for s in range(LOOPS_DEV)], axis=1)
    spec = nn_dot(loops.astype(BF16), sorted_s[...])
    spec = jnp.where(iota((8, WAVES), 1) < WAVES - own, spec, 0.0).astype(BF16).astype(F32)
    wide = jnp.broadcast_to(spec[:, None, :], (8, ROWS_DEV, WAVES)).reshape(8 * ROWS_DEV, WAVES)
    ri = iota((8 * ROWS_DEV, WAVES), 0) & (ROWS_DEV - 1)
    wide = jnp.concatenate([jnp.where(ri == r, wide, 0.0) for r in range(ROWS_DEV)], axis=1)
    wide = jnp.concatenate([wide, wide], axis=0).astype(BF16)
    send2[...] = nt_dot(syn_s[...], wide).astype(BF16).astype(F32)

    def row_of(to):
        return send2.at[pl.ds(to, 1)]

    def push_row(to):
        push(row_of(to), recv2.at[pl.ds(gx, 1)], 1, x, to)

    def push_far(to):
        for d in (2, 1, 3, 0):
            push(row_of(to), far2.at[x, pl.ds(gx, 1)], 3, (x + d) & (NX - 1), to)

    @pl.loop(0, FAR)
    def _(k):
        tz = (z + farthest_first(k, NZ // 2)) & (NZ - 1)

        @pl.when(tz < EARLY)
        def _():
            near(tz, NYC, push_far)

        @pl.when(tz >= EARLY)
        def _():
            near(tz, NYC, push_row)

    @pl.loop(FAR, NZ - 1)
    def _(k):
        near((z + farthest_first(k, NZ // 2)) & (NZ - 1), NYC, push_row)

    near(z, NYC - 1, push_row)
    pltpu.make_async_copy(row_of(gx), recv2.at[pl.ds(gx, 1)], recv_sem.at[1]).start()
    wave_s[...] = jnp.broadcast_to(wave.astype(F32), (WAVES, WAVES)).T.astype(I32) + FIRST_WAVE
    lon_start = x * LON_DEV

    @pl.loop(0, NGX // 16)
    def _(i):
        at = pl.ds(pl.multiple_of(i * 16, 16), 16)
        col = wave_s[at, :]
        for n in range(0, LON_PAD, LANES):
            lon = iota((16, LANES), 1) + (lon_start + n)
            cos, sin = table_tile(col, lon)
            table_s[0, at, n : n + LANES] = cos
            table_s[1, at, n : n + LANES] = sin

    local[5].wait()
    local[6].wait()

    @pl.when(early)
    def _():
        wait_all(recv2.at[pl.ds(0, (NZ - FAR) * NYC)], recv_sem.at[1])

    @pl.when(jnp.logical_not(early))
    def _():
        wait_all(recv2, recv_sem.at[1])

    half = 4 * ROWS_DEV
    send3[...] = recv2[...].T[: 2 * half].astype(BF16)
    for d in (2, 1, 3):
        push(send3, recv3.at[x], 2, (x + d) & (NX - 1), gx)
    pltpu.make_async_copy(send3, recv3.at[x], recv_sem.at[2]).start()

    def set_rows(v, block):
        at = slice(v * half, (v + 1) * half)
        rows_s[at, :NGX] = block[:half]
        rows_s[at, NGX:] = block[half:]

    @pl.when(early)
    def _():
        wait_all(far2.at[:, pl.ds(0, FAR * NYC)], recv_sem.at[3])
        wait_all(recv3, recv_sem.at[2])
        first = iota((NGX, LANES), 1) < 2 * half
        for v in range(0, NX, 2):
            both = jnp.where(first, far2[v], far2[v + 1]).T
            for i in range(2):
                far = both[2 * half * i : 2 * half * (i + 1)]
                set_rows(v + i, (recv3[v + i].astype(F32) + far).astype(BF16))

    @pl.when(jnp.logical_not(early))
    def _():
        wait_all(recv3, recv_sem.at[2])
        for v in range(NX):
            set_rows(v, recv3[v])

    rows = rows_s[...]
    for n in range(0, LON_DEV, 2 * LANES):
        table = table_s[:, :, n : n + 2 * LANES].reshape(2 * NGX, 2 * LANES)
        field = nn_dot(rows, table).reshape(LEV, ROWS_DEV, 2 * LANES)
        for k in range(n, min(n + 2 * LANES, LON_DEV), LANES):
            width = min(LANES, LON_DEV - k)
            levels = [field[v, :, k - n : k - n + width] for v in range(LEV)]
            for p in range(POUT):
                below = bracket_v[p, :, k : k + width]
                weight = frac_v[p, :, k : k + width]
                low, high = two_levels(levels, below)
                out_ref[p, :, k : k + width] = (1.0 - weight) * low + weight * high

    wait_all(send1.at[pl.ds(0, NGX - 1)], send_sem.at[0])
    wait_all(send2.at[pl.ds(0, NGX - 1 - NYC * EARLY)], send_sem.at[1])
    for tz in range(EARLY):
        away = (tz - z) & (NZ - 1)
        is_far = jnp.abs(away - NZ // 2) <= FAR // 2

        @pl.when(is_far)
        def _():
            wait_all(far2.at[0, pl.ds(0, NX * NYC)], send_sem.at[3])

        @pl.when(jnp.logical_not(is_far))
        def _():
            wait_all(send2.at[pl.ds(0, NYC)], send_sem.at[1])

    wait_all(recv3.at[pl.ds(0, NX - 1)], send_sem.at[2])


def shards(fourier, lat_of_row, wave_order, analysis, synthesis, bracket, frac):
    lat = lat_of_row.reshape(LOOPS_DEV, LANES)
    wave = wave_order.reshape(1, WAVES)
    fourier = jnp.transpose(fourier, (1, 3, 2, 0))
    vmem = pl.BlockSpec(memory_space=pltpu.VMEM)
    hbm = pl.BlockSpec(memory_space=pltpu.HBM)
    return pl.pallas_call(
        kernel,
        out_shape=pltpu.VMEM((POUT, ROWS_DEV, LON_DEV), F32),
        in_specs=[hbm] * 7,
        out_specs=vmem,
        scratch_shapes=[
            pltpu.VMEM((2, LOOPS_DEV, LEV_DEV, WAVES), BF16),
            pltpu.VMEM((1, WAVES), I32),
            pltpu.VMEM((LOOPS_DEV, LANES), I32),
            pltpu.VMEM((WAVES, HALF), BF16),
            pltpu.VMEM((NGX * ROWS_DEV, WAVES), BF16),
            pltpu.VMEM((POUT, ROWS_DEV, LON_DEV), I32),
            pltpu.VMEM((POUT, ROWS_DEV, LON_DEV), F32),
            pltpu.VMEM((NGX, 2, LANES), BF16),
            pltpu.VMEM((NGX, 2, LANES), BF16),
            pltpu.VMEM((NGX, LANES), F32),
            pltpu.VMEM((NGX, LANES), F32),
            pltpu.VMEM((8 * ROWS_DEV, NGX), BF16),
            pltpu.VMEM((NX, 8 * ROWS_DEV, NGX), BF16),
            pltpu.VMEM((NX, NGX, LANES), F32),
            pltpu.VMEM((LEV * ROWS_DEV, 2 * NGX), BF16),
            pltpu.VMEM((2, 24, LANES), I32),
            pltpu.VMEM((NLAT, WAVES), BF16),
            pltpu.VMEM((2 * NGX, LANES), F32),
            pltpu.VMEM((NGX * ROWS_DEV, WAVES), F32),
            pltpu.VMEM((NGX, ROWS_DEV * WAVES), BF16),
            pltpu.VMEM((WAVES, LANES), I32),
            pltpu.VMEM((2, NGX, LON_PAD), BF16),
            pltpu.VMEM((LEV, ROWS_DEV, LON_PAD), F32),
            pltpu.SemaphoreType.DMA((7,)),
            pltpu.SemaphoreType.DMA((4,)),
            pltpu.SemaphoreType.DMA((4,)),
        ],
        compiler_params=pltpu.CompilerParams(
            collective_id=0, has_side_effects=True, vmem_limit_bytes=56 * 1024 * 1024
        ),
        cost_estimate=pl.CostEstimate(flops=10**9, bytes_accessed=1400000, transcendentals=0),
    )(
        fourier, wave, lat, analysis.reshape(WAVES, HALF),
        synthesis.reshape(NGX * ROWS_DEV, WAVES), bracket, frac,
    )


def solution(mesh):
    placed = (
        P(None, None, "grp", "gx"),
        P(),
        P(),
        P("gx", None, None),
        P("gx", None, None),
        P(None, "gx", "grp"),
        P(None, "gx", "grp"),
    )
    return jax.shard_map(
        shards, mesh=mesh, in_specs=placed, out_specs=P(None, "gx", "grp"), check_vma=False
    )
```

```python
import functools
import math

import jax
import jax.numpy as jnp
from jax import lax
from jax.experimental import pallas as pl
from jax.experimental.pallas import tpu as pltpu
from jax.sharding import PartitionSpec as P

MESH = pl.DeviceIdType.MESH
F32, BF16, I32 = jnp.float32, jnp.bfloat16, jnp.int32

NX, NZ, NYC = 4, 16, 8
NGX = NZ * NYC
MTOT, NLAT, NLON = 1280, 2560, 3600
WAVES = 128
FIRST_WAVE = MTOT - WAVES
LEV_DEV, ROWS_DEV, LOOPS_DEV, LON_DEV, POUT, LEV = 4, 8, 20, 900, 8, 16
HALF = NLAT // 2
LANES = 128
LON_PAD = 1024
FIRST = 4
TABLE_SOON = 5
EARLY = 3
FAR = 5


def iota(shape, axis):
    return lax.broadcasted_iota(I32, shape, axis)


def nt_dot(a, b):
    return lax.dot_general(a, b, (((1,), (1,)), ((), ())), preferred_element_type=F32)


def nn_dot(a, b):
    return lax.dot_general(a, b, (((1,), (0,)), ((), ())), preferred_element_type=F32)


def ordered_waves(fourier, wave):
    pick = (iota((WAVES, WAVES), 0) == wave).astype(F32)
    pick = pick.T.astype(BF16)
    rows = jnp.concatenate([fourier[0].astype(F32), fourier[1].astype(F32)], axis=1)
    rows = rows.reshape(LOOPS_DEV * 8, WAVES)
    rows = jnp.concatenate([rows, jnp.zeros((256 - LOOPS_DEV * 8, WAVES), F32)], axis=0)
    return nt_dot(pick, rows.astype(BF16))


def loop_lats(lat):
    flat = iota((24, LANES), 1) * LOOPS_DEV + jnp.minimum(iota((24, LANES), 0), LOOPS_DEV - 1)
    high, low = flat >> 7, flat & (LANES - 1)
    out = jnp.zeros((24, LANES), I32)
    for a in range(LOOPS_DEV):
        row = jnp.broadcast_to(lat[a : a + 1], (24, LANES))
        out = jnp.where(high == a, jnp.take_along_axis(row, low, axis=1), out)
    return out


def table_tile(wave_col, lon):
    turns = wave_col * lon
    quarter = jnp.floor(turns.astype(F32) * (4.0 / NLON) + 0.5).astype(I32)
    rest = (turns - quarter * (NLON // 4)).astype(F32) * (2.0 * math.pi / NLON)
    sq = rest * rest
    c = 1.0 + sq * (-0.5 + sq * (1.0 / 24 + sq * (-1.0 / 720 + sq * (1.0 / 40320))))
    s = rest * (1.0 + sq * (-1.0 / 6 + sq * (1.0 / 120 + sq * (-1.0 / 5040 + sq * (1.0 / 362880)))))
    odd = (quarter & 1) == 1
    cos = jnp.where(odd, s, c)
    sin = jnp.where(odd, c, s)
    cos = jnp.where(((quarter + 1) & 2) == 2, -2.0 * cos, 2.0 * cos)
    sin = jnp.where((quarter & 2) == 2, 2.0 * sin, -2.0 * sin)
    return cos.astype(BF16), sin.astype(BF16)


def one_level(levels, bits):
    for bit in bits:
        levels = [jnp.where(bit, b, a) for a, b in zip(levels[0::2], levels[1::2])]
    return levels[0]


def two_levels(levels, below):
    bits = [(below & (1 << i)) != 0 for i in range(4)]

    def pair(values, bits):
        if not bits:
            return values[0], values[1]
        even, after = pair(values[0::2], bits[1:])
        odd = one_level(values[1::2], bits[1:])
        return jnp.where(bits[0], odd, even), jnp.where(bits[0], after, odd)

    return pair(levels + levels[-1:], bits)


def farthest_first(step, half):
    return half + ((step + 1) >> 1) * (1 - 2 * (step & 1))


def kernel(
    fourier_ref, wave_ref, lat_ref, analysis_ref, synthesis_ref, bracket_ref, frac_ref,
    out_ref,
    fourier_v, wave_v, lat_v, analysis_v, synthesis_v, bracket_v, frac_v,
    send1, recv1, send2, recv2, send3, recv3, far2, rows_s,
    lats_s, sorted_s, spread_s, syn_f, syn_s, wave_s, table_s, field_s,
    local_sem, send_sem, recv_sem,
):
    x = lax.axis_index("grp")
    gx = lax.axis_index("gx")
    z, yc = gx >> 3, gx & (NYC - 1)

    def near(tz, count, action):
        for j in range(count):
            action((tz << 3) + ((yc + farthest_first(j, NYC // 2)) & (NYC - 1)))

    def peers(action):
        @pl.loop(0, NZ - 1)
        def _(k):
            near((z + farthest_first(k, NZ // 2)) & (NZ - 1), NYC, action)

        near(z, NYC - 1, action)

    early = z < EARLY

    @pl.when(early)
    def _():
        recv2[...] = jnp.zeros((NGX, LANES), F32)
        far2[...] = jnp.zeros((NX, NGX, LANES), F32)

    barrier = pltpu.get_barrier_semaphore()

    def signal(tx, to):
        pl.semaphore_signal(barrier, inc=1, device_id=(tx, to), device_id_type=MESH)

    peers(lambda to: signal(x, to))
    for d in (2, 1, 3):
        signal((x + d) & (NX - 1), gx)

    local = [
        pltpu.make_async_copy(src, dst, local_sem.at[i])
        for i, (src, dst) in enumerate(
            (
                (fourier_ref, fourier_v),
                (wave_ref, wave_v),
                (lat_ref, lat_v),
                (analysis_ref, analysis_v),
                (synthesis_ref, synthesis_v),
                (bracket_ref, bracket_v),
                (frac_ref, frac_v),
            )
        )
    ]
    for copy in local:
        copy.start()

    def push(src, dst, stage, tx, to):
        pltpu.make_async_remote_copy(
            src_ref=src,
            dst_ref=dst,
            send_sem=send_sem.at[stage],
            recv_sem=recv_sem.at[stage],
            device_id=(tx, to),
            device_id_type=MESH,
        ).start()

    def wait_all(ref, sem):
        pltpu.make_async_copy(ref, ref, sem).wait()

    local[0].wait()
    local[1].wait()
    wave = wave_v[...]
    ordered = ordered_waves(fourier_v[...], wave)
    spread_s[pl.ds(0, NGX, stride=2), :] = ordered[:, :LANES]
    spread_s[pl.ds(1, NGX, stride=2), :] = ordered[:, LANES:]
    send1.reshape(2 * NGX, LANES)[...] = spread_s[...].astype(BF16)
    pl.semaphore_wait(barrier, NGX - 1 + NX - 1)
    peers(lambda to: push(send1.at[to], recv1.at[gx], 0, x, to))
    pltpu.make_async_copy(send1.at[gx], recv1.at[gx], recv_sem.at[0]).start()

    local[2].wait()
    lats = loop_lats(lat_v[...])
    own = jnp.sum(jnp.where(iota((1, WAVES), 1) == gx, wave, 0), axis=1, keepdims=True)
    pole = jnp.minimum(lats, NLAT - 1 - lats)
    live = 2 * (FIRST_WAVE + own) < 20 + 4 * pole
    lats_s[0] = jnp.where(live, pole, -1)
    lats_s[1] = jnp.where(lats >= HALF, 1, 0)
    local[3].wait()

    @pl.loop(0, LOOPS_DEV // 2)
    def _(pair):
        row = lats_s[0, pl.ds(2 * pair, 2), :]
        south = lats_s[1, pl.ds(2 * pair, 2), :]
        row = jnp.concatenate([row[0:1], row[1:2]], axis=1)
        south = jnp.concatenate([south[0:1], south[1:2]], axis=1)
        total = jnp.zeros((WAVES, 2 * LANES), F32)
        for j in range(0, HALF, 256):
            hot = (iota((256, 2 * LANES), 0) + j == row).astype(F32).astype(BF16)
            total += nn_dot(analysis_v[:, j : j + 256], hot)
        odd = iota((WAVES, 2 * LANES), 0) & 1
        total = jnp.where((odd * south) == 1, -total, total)
        sorted_s[pl.ds(pl.multiple_of(pair * 256, 256), 256), :] = total.T.astype(BF16)

    local[4].wait()
    syn_f[...] = synthesis_v[...].astype(F32)
    for ri in range(ROWS_DEV):
        syn_s[:, ri * LANES : (ri + 1) * LANES] = syn_f[pl.ds(ri, NGX, stride=ROWS_DEV), :].astype(BF16)

    wait_all(recv1, recv_sem.at[0])
    spread_s[...] = recv1.reshape(2 * NGX, LANES)[...].astype(F32)
    head = spread_s[pl.ds(0, NGX, stride=2), :].T
    tail = spread_s[pl.ds(1, NGX, stride=2), :].T
    loops = jnp.concatenate([head, tail], axis=0)
    loops = jnp.concatenate([loops[8 * s : 8 * s + 8] for s in range(LOOPS_DEV)], axis=1)
    spec = nn_dot(loops.astype(BF16), sorted_s[...])
    spec = jnp.where(iota((8, WAVES), 1) < WAVES - own, spec, 0.0).astype(BF16).astype(F32)
    wide = jnp.broadcast_to(spec[:, None, :], (8, ROWS_DEV, WAVES)).reshape(8 * ROWS_DEV, WAVES)
    ri = iota((8 * ROWS_DEV, WAVES), 0) & (ROWS_DEV - 1)
    wide = jnp.concatenate([jnp.where(ri == r, wide, 0.0) for r in range(ROWS_DEV)], axis=1)
    wide = jnp.concatenate([wide, wide], axis=0).astype(BF16)
    send2[...] = nt_dot(syn_s[...], wide).astype(BF16).astype(F32)

    def row_of(to):
        return send2.at[pl.ds(to, 1)]

    def push_row(to):
        push(row_of(to), recv2.at[pl.ds(gx, 1)], 1, x, to)

    def push_far(to):
        for d in (2, 1, 3, 0):
            push(row_of(to), far2.at[x, pl.ds(gx, 1)], 3, (x + d) & (NX - 1), to)

    def push_plane(tz):
        is_far = jnp.abs(((tz - z) & (NZ - 1)) - NZ // 2) <= FAR // 2
        at_once = jnp.logical_and(is_far, tz < EARLY)

        @pl.when(at_once)
        def _():
            near(tz, NYC, push_far)

        @pl.when(jnp.logical_and(jnp.logical_not(at_once), tz != z))
        def _():
            near(tz, NYC, push_row)

    pl.loop(0, FIRST)(push_plane)
    wave_s[...] = jnp.broadcast_to(wave.astype(F32), (WAVES, WAVES)).T.astype(I32) + FIRST_WAVE
    lon_start = x * LON_DEV

    def table_rows(i):
        at = pl.ds(pl.multiple_of(i * 16, 16), 16)
        col = wave_s[at, :]
        for n in range(0, LON_PAD, LANES):
            lon = iota((16, LANES), 1) + (lon_start + n)
            cos, sin = table_tile(col, lon)
            table_s[0, at, n : n + LANES] = cos
            table_s[1, at, n : n + LANES] = sin

    pl.loop(0, TABLE_SOON)(table_rows)
    pl.loop(FIRST, NZ)(push_plane)
    near(z, NYC - 1, push_row)
    pltpu.make_async_copy(row_of(gx), recv2.at[pl.ds(gx, 1)], recv_sem.at[1]).start()
    pl.loop(TABLE_SOON, NGX // 16)(table_rows)
    local[5].wait()
    local[6].wait()

    @pl.when(early)
    def _():
        wait_all(recv2.at[pl.ds(0, (NZ - FAR) * NYC)], recv_sem.at[1])

    @pl.when(jnp.logical_not(early))
    def _():
        wait_all(recv2, recv_sem.at[1])

    half = 4 * ROWS_DEV
    send3[...] = recv2[...].T[: 2 * half].astype(BF16)
    for d in (2, 1, 3):
        push(send3, recv3.at[x], 2, (x + d) & (NX - 1), gx)
    pltpu.make_async_copy(send3, recv3.at[x], recv_sem.at[2]).start()

    def set_rows(v, block):
        at = slice(v * half, (v + 1) * half)
        rows_s[at, :NGX] = block[:half]
        rows_s[at, NGX:] = block[half:]

    @pl.when(early)
    def _():
        wait_all(far2.at[:, pl.ds(0, FAR * NYC)], recv_sem.at[3])
        wait_all(recv3, recv_sem.at[2])
        first = iota((NGX, LANES), 1) < 2 * half
        for v in range(0, NX, 2):
            both = jnp.where(first, far2[v], far2[v + 1]).T
            for i in range(2):
                far = both[2 * half * i : 2 * half * (i + 1)]
                set_rows(v + i, (recv3[v + i].astype(F32) + far).astype(BF16))

    @pl.when(jnp.logical_not(early))
    def _():
        wait_all(recv3, recv_sem.at[2])
        for v in range(NX):
            set_rows(v, recv3[v])

    rows = rows_s[...]
    for n in range(0, LON_DEV, 2 * LANES):
        table = table_s[:, :, n : n + 2 * LANES].reshape(2 * NGX, 2 * LANES)
        field = nn_dot(rows, table).reshape(LEV, ROWS_DEV, 2 * LANES)
        for k in range(n, min(n + 2 * LANES, LON_DEV), LANES):
            width = min(LANES, LON_DEV - k)
            levels = [field[v, :, k - n : k - n + width] for v in range(LEV)]
            for p in range(POUT):
                below = bracket_v[p, :, k : k + width]
                weight = frac_v[p, :, k : k + width]
                low, high = two_levels(levels, below)
                out_ref[p, :, k : k + width] = (1.0 - weight) * low + weight * high

    wait_all(send1.at[pl.ds(0, NGX - 1)], send_sem.at[0])
    wait_all(send2.at[pl.ds(0, NGX - 1 - NYC * EARLY)], send_sem.at[1])
    for tz in range(EARLY):
        away = (tz - z) & (NZ - 1)
        is_far = jnp.abs(away - NZ // 2) <= FAR // 2

        @pl.when(is_far)
        def _():
            wait_all(far2.at[0, pl.ds(0, NX * NYC)], send_sem.at[3])

        @pl.when(jnp.logical_not(is_far))
        def _():
            wait_all(send2.at[pl.ds(0, NYC)], send_sem.at[1])

    wait_all(recv3.at[pl.ds(0, NX - 1)], send_sem.at[2])


def shards(fourier, lat_of_row, wave_order, analysis, synthesis, bracket, frac):
    lat = lat_of_row.reshape(LOOPS_DEV, LANES)
    wave = wave_order.reshape(1, WAVES)
    fourier = jnp.transpose(fourier, (1, 3, 2, 0))
    vmem = pl.BlockSpec(memory_space=pltpu.VMEM)
    hbm = pl.BlockSpec(memory_space=pltpu.HBM)
    return pl.pallas_call(
        kernel,
        out_shape=pltpu.VMEM((POUT, ROWS_DEV, LON_DEV), F32),
        in_specs=[hbm] * 7,
        out_specs=vmem,
        scratch_shapes=[
            pltpu.VMEM((2, LOOPS_DEV, LEV_DEV, WAVES), BF16),
            pltpu.VMEM((1, WAVES), I32),
            pltpu.VMEM((LOOPS_DEV, LANES), I32),
            pltpu.VMEM((WAVES, HALF), BF16),
            pltpu.VMEM((NGX * ROWS_DEV, WAVES), BF16),
            pltpu.VMEM((POUT, ROWS_DEV, LON_DEV), I32),
            pltpu.VMEM((POUT, ROWS_DEV, LON_DEV), F32),
            pltpu.VMEM((NGX, 2, LANES), BF16),
            pltpu.VMEM((NGX, 2, LANES), BF16),
            pltpu.VMEM((NGX, LANES), F32),
            pltpu.VMEM((NGX, LANES), F32),
            pltpu.VMEM((8 * ROWS_DEV, NGX), BF16),
            pltpu.VMEM((NX, 8 * ROWS_DEV, NGX), BF16),
            pltpu.VMEM((NX, NGX, LANES), F32),
            pltpu.VMEM((LEV * ROWS_DEV, 2 * NGX), BF16),
            pltpu.VMEM((2, 24, LANES), I32),
            pltpu.VMEM((NLAT, WAVES), BF16),
            pltpu.VMEM((2 * NGX, LANES), F32),
            pltpu.VMEM((NGX * ROWS_DEV, WAVES), F32),
            pltpu.VMEM((NGX, ROWS_DEV * WAVES), BF16),
            pltpu.VMEM((WAVES, LANES), I32),
            pltpu.VMEM((2, NGX, LON_PAD), BF16),
            pltpu.VMEM((LEV, ROWS_DEV, LON_PAD), F32),
            pltpu.SemaphoreType.DMA((7,)),
            pltpu.SemaphoreType.DMA((4,)),
            pltpu.SemaphoreType.DMA((4,)),
        ],
        compiler_params=pltpu.CompilerParams(
            collective_id=0, has_side_effects=True, vmem_limit_bytes=56 * 1024 * 1024
        ),
        cost_estimate=pl.CostEstimate(flops=10**9, bytes_accessed=1400000, transcendentals=0),
    )(
        fourier, wave, lat, analysis.reshape(WAVES, HALF),
        synthesis.reshape(NGX * ROWS_DEV, WAVES), bracket, frac,
    )


def solution(mesh):
    placed = (
        P(None, None, "grp", "gx"),
        P(),
        P(),
        P("gx", None, None),
        P("gx", None, None),
        P(None, "gx", "grp"),
        P(None, "gx", "grp"),
    )
    return jax.shard_map(
        shards, mesh=mesh, in_specs=placed, out_specs=P(None, "gx", "grp"), check_vma=False
    )
```

```python
import functools
import math

import jax
import jax.numpy as jnp
from jax import lax
from jax.experimental import pallas as pl
from jax.experimental.pallas import tpu as pltpu
from jax.sharding import PartitionSpec as P

MESH = pl.DeviceIdType.MESH
F32, BF16, I32 = jnp.float32, jnp.bfloat16, jnp.int32

NX, NZ, NYC = 4, 16, 8
NGX = NZ * NYC
MTOT, NLAT, NLON = 1280, 2560, 3600
WAVES = 128
FIRST_WAVE = MTOT - WAVES
LEV_DEV, ROWS_DEV, LOOPS_DEV, LON_DEV, POUT, LEV = 4, 8, 20, 900, 8, 16
HALF = NLAT // 2
LANES = 128
LON_PAD = 1024
FIRST = 4
TABLE_SOON = 5
EARLY = 3
FAR = 5


def iota(shape, axis):
    return lax.broadcasted_iota(I32, shape, axis)


def nt_dot(a, b):
    return lax.dot_general(a, b, (((1,), (1,)), ((), ())), preferred_element_type=F32)


def nn_dot(a, b):
    return lax.dot_general(a, b, (((1,), (0,)), ((), ())), preferred_element_type=F32)


def ordered_waves(fourier, wave):
    pick = (iota((WAVES, WAVES), 0) == wave).astype(F32)
    pick = pick.T.astype(BF16)
    rows = jnp.concatenate([fourier[0].astype(F32), fourier[1].astype(F32)], axis=1)
    rows = rows.reshape(LOOPS_DEV * 8, WAVES)
    rows = jnp.concatenate([rows, jnp.zeros((256 - LOOPS_DEV * 8, WAVES), F32)], axis=0)
    return nt_dot(pick, rows.astype(BF16))


def loop_lats(lat):
    flat = iota((24, LANES), 1) * LOOPS_DEV + jnp.minimum(iota((24, LANES), 0), LOOPS_DEV - 1)
    high, low = flat >> 7, flat & (LANES - 1)
    out = jnp.zeros((24, LANES), I32)
    for a in range(LOOPS_DEV):
        row = jnp.broadcast_to(lat[a : a + 1], (24, LANES))
        out = jnp.where(high == a, jnp.take_along_axis(row, low, axis=1), out)
    return out


def table_tile(wave_col, lon):
    turns = wave_col * lon
    quarter = jnp.floor(turns.astype(F32) * (4.0 / NLON) + 0.5).astype(I32)
    rest = (turns - quarter * (NLON // 4)).astype(F32) * (2.0 * math.pi / NLON)
    sq = rest * rest
    c = 1.0 + sq * (-0.5 + sq * (1.0 / 24 + sq * (-1.0 / 720 + sq * (1.0 / 40320))))
    s = rest * (1.0 + sq * (-1.0 / 6 + sq * (1.0 / 120 + sq * (-1.0 / 5040 + sq * (1.0 / 362880)))))
    odd = (quarter & 1) == 1
    cos = jnp.where(odd, s, c)
    sin = jnp.where(odd, c, s)
    cos = jnp.where(((quarter + 1) & 2) == 2, -2.0 * cos, 2.0 * cos)
    sin = jnp.where((quarter & 2) == 2, 2.0 * sin, -2.0 * sin)
    return cos.astype(BF16), sin.astype(BF16)


def one_level(levels, bits):
    for bit in bits:
        levels = [jnp.where(bit, b, a) for a, b in zip(levels[0::2], levels[1::2])]
    return levels[0]


def two_levels(levels, below):
    bits = [(below & (1 << i)) != 0 for i in range(4)]

    def pair(values, bits):
        if not bits:
            return values[0], values[1]
        even, after = pair(values[0::2], bits[1:])
        odd = one_level(values[1::2], bits[1:])
        return jnp.where(bits[0], odd, even), jnp.where(bits[0], after, odd)

    return pair(levels + levels[-1:], bits)


def farthest_first(step, half):
    return half + ((step + 1) >> 1) * (1 - 2 * (step & 1))


def kernel(
    fourier_ref, wave_ref, lat_ref, analysis_ref, synthesis_ref, bracket_ref, frac_ref,
    out_ref,
    fourier_v, wave_v, lat_v, analysis_v, synthesis_v, bracket_v, frac_v,
    send1, recv1, send2, recv2, send3, recv3, far2, far_s, rows_s,
    lats_s, sorted_s, spread_s, syn_f, syn_s, wave_s, table_s, field_s,
    local_sem, send_sem, recv_sem,
):
    x = lax.axis_index("grp")
    gx = lax.axis_index("gx")
    z, yc = gx >> 3, gx & (NYC - 1)

    def near(tz, count, action):
        for j in range(count):
            action((tz << 3) + ((yc + farthest_first(j, NYC // 2)) & (NYC - 1)))

    def peers(action):
        @pl.loop(0, NZ - 1)
        def _(k):
            near((z + farthest_first(k, NZ // 2)) & (NZ - 1), NYC, action)

        near(z, NYC - 1, action)

    early = z < EARLY

    @pl.when(early)
    def _():
        recv2[...] = jnp.zeros((NGX, LANES), F32)
        far2[...] = jnp.zeros((NX, NGX, LANES), F32)

    barrier = pltpu.get_barrier_semaphore()

    def signal(tx, to):
        pl.semaphore_signal(barrier, inc=1, device_id=(tx, to), device_id_type=MESH)

    peers(lambda to: signal(x, to))
    for d in (2, 1, 3):
        signal((x + d) & (NX - 1), gx)

    local = [
        pltpu.make_async_copy(src, dst, local_sem.at[i])
        for i, (src, dst) in enumerate(
            (
                (fourier_ref, fourier_v),
                (wave_ref, wave_v),
                (lat_ref, lat_v),
                (analysis_ref, analysis_v),
                (synthesis_ref, synthesis_v),
                (bracket_ref, bracket_v),
                (frac_ref, frac_v),
            )
        )
    ]
    for copy in local:
        copy.start()

    def push(src, dst, stage, tx, to):
        pltpu.make_async_remote_copy(
            src_ref=src,
            dst_ref=dst,
            send_sem=send_sem.at[stage],
            recv_sem=recv_sem.at[stage],
            device_id=(tx, to),
            device_id_type=MESH,
        ).start()

    def wait_all(ref, sem):
        pltpu.make_async_copy(ref, ref, sem).wait()

    local[0].wait()
    local[1].wait()
    wave = wave_v[...]
    ordered = ordered_waves(fourier_v[...], wave)
    spread_s[pl.ds(0, NGX, stride=2), :] = ordered[:, :LANES]
    spread_s[pl.ds(1, NGX, stride=2), :] = ordered[:, LANES:]
    send1.reshape(2 * NGX, LANES)[...] = spread_s[...].astype(BF16)
    pl.semaphore_wait(barrier, NGX - 1 + NX - 1)
    peers(lambda to: push(send1.at[to], recv1.at[gx], 0, x, to))
    pltpu.make_async_copy(send1.at[gx], recv1.at[gx], recv_sem.at[0]).start()

    local[2].wait()
    lats = loop_lats(lat_v[...])
    own = jnp.sum(jnp.where(iota((1, WAVES), 1) == gx, wave, 0), axis=1, keepdims=True)
    pole = jnp.minimum(lats, NLAT - 1 - lats)
    live = 2 * (FIRST_WAVE + own) < 20 + 4 * pole
    lats_s[0] = jnp.where(live, pole, -1)
    lats_s[1] = jnp.where(lats >= HALF, 1, 0)
    local[3].wait()

    @pl.loop(0, LOOPS_DEV // 2)
    def _(pair):
        row = lats_s[0, pl.ds(2 * pair, 2), :]
        south = lats_s[1, pl.ds(2 * pair, 2), :]
        row = jnp.concatenate([row[0:1], row[1:2]], axis=1)
        south = jnp.concatenate([south[0:1], south[1:2]], axis=1)
        total = jnp.zeros((WAVES, 2 * LANES), F32)
        for j in range(0, HALF, 256):
            hot = (iota((256, 2 * LANES), 0) + j == row).astype(F32).astype(BF16)
            total += nn_dot(analysis_v[:, j : j + 256], hot)
        odd = iota((WAVES, 2 * LANES), 0) & 1
        total = jnp.where((odd * south) == 1, -total, total)
        sorted_s[pl.ds(pl.multiple_of(pair * 256, 256), 256), :] = total.T.astype(BF16)

    local[4].wait()
    syn_f[...] = synthesis_v[...].astype(F32)
    for ri in range(ROWS_DEV):
        syn_s[:, ri * LANES : (ri + 1) * LANES] = syn_f[pl.ds(ri, NGX, stride=ROWS_DEV), :].astype(BF16)

    wait_all(recv1, recv_sem.at[0])
    spread_s[...] = recv1.reshape(2 * NGX, LANES)[...].astype(F32)
    head = spread_s[pl.ds(0, NGX, stride=2), :].T
    tail = spread_s[pl.ds(1, NGX, stride=2), :].T
    loops = jnp.concatenate([head, tail], axis=0)
    loops = jnp.concatenate([loops[8 * s : 8 * s + 8] for s in range(LOOPS_DEV)], axis=1)
    spec = nn_dot(loops.astype(BF16), sorted_s[...])
    spec = jnp.where(iota((8, WAVES), 1) < WAVES - own, spec, 0.0).astype(BF16).astype(F32)
    wide = jnp.broadcast_to(spec[:, None, :], (8, ROWS_DEV, WAVES)).reshape(8 * ROWS_DEV, WAVES)
    ri = iota((8 * ROWS_DEV, WAVES), 0) & (ROWS_DEV - 1)
    wide = jnp.concatenate([jnp.where(ri == r, wide, 0.0) for r in range(ROWS_DEV)], axis=1)
    wide = jnp.concatenate([wide, wide], axis=0).astype(BF16)
    send2[...] = nt_dot(syn_s[...], wide).astype(BF16).astype(F32)

    def row_of(to):
        return send2.at[pl.ds(to, 1)]

    def push_row(to):
        push(row_of(to), recv2.at[pl.ds(gx, 1)], 1, x, to)

    def push_far(to):
        for d in (2, 1, 3, 0):
            push(row_of(to), far2.at[x, pl.ds(gx, 1)], 3, (x + d) & (NX - 1), to)

    def push_plane(tz):
        is_far = jnp.abs(((tz - z) & (NZ - 1)) - NZ // 2) <= FAR // 2
        at_once = jnp.logical_and(is_far, tz < EARLY)

        @pl.when(at_once)
        def _():
            near(tz, NYC, push_far)

        @pl.when(jnp.logical_and(jnp.logical_not(at_once), tz != z))
        def _():
            near(tz, NYC, push_row)

    pl.loop(0, FIRST)(push_plane)
    wave_s[...] = jnp.broadcast_to(wave.astype(F32), (WAVES, WAVES)).T.astype(I32) + FIRST_WAVE
    lon_start = x * LON_DEV

    def table_rows(i):
        at = pl.ds(pl.multiple_of(i * 16, 16), 16)
        col = wave_s[at, :]
        for n in range(0, LON_PAD, LANES):
            lon = iota((16, LANES), 1) + (lon_start + n)
            cos, sin = table_tile(col, lon)
            table_s[0, at, n : n + LANES] = cos
            table_s[1, at, n : n + LANES] = sin

    pl.loop(0, TABLE_SOON)(table_rows)
    pl.loop(FIRST, NZ)(push_plane)
    near(z, NYC - 1, push_row)
    pltpu.make_async_copy(row_of(gx), recv2.at[pl.ds(gx, 1)], recv_sem.at[1]).start()
    pl.loop(TABLE_SOON, NGX // 16)(table_rows)
    local[5].wait()
    local[6].wait()

    @pl.when(early)
    def _():
        wait_all(recv2.at[pl.ds(0, (NZ - FAR) * NYC)], recv_sem.at[1])

    @pl.when(jnp.logical_not(early))
    def _():
        wait_all(recv2, recv_sem.at[1])

    half = 4 * ROWS_DEV
    send3[...] = recv2[...].T[: 2 * half].astype(BF16)
    for d in (2, 1, 3):
        push(send3, recv3.at[x], 2, (x + d) & (NX - 1), gx)
    pltpu.make_async_copy(send3, recv3.at[x], recv_sem.at[2]).start()

    def set_rows(v, block):
        at = slice(v * half, (v + 1) * half)
        rows_s[at, :NGX] = block[:half]
        rows_s[at, NGX:] = block[half:]

    @pl.when(early)
    def _():
        wait_all(far2.at[:, pl.ds(0, FAR * NYC)], recv_sem.at[3])
        first = iota((NGX, LANES), 1) < 2 * half
        for v in range(0, NX, 2):
            both = jnp.where(first, far2[v], far2[v + 1]).T
            far_s[2 * half * v : 2 * half * (v + 2), :] = both
        wait_all(recv3, recv_sem.at[2])
        for v in range(NX):
            far = far_s[2 * half * v : 2 * half * (v + 1), :]
            set_rows(v, (recv3[v].astype(F32) + far).astype(BF16))

    @pl.when(jnp.logical_not(early))
    def _():
        wait_all(recv3, recv_sem.at[2])
        for v in range(NX):
            set_rows(v, recv3[v])

    rows = rows_s[...]
    for n in range(0, LON_DEV, 2 * LANES):
        table = table_s[:, :, n : n + 2 * LANES].reshape(2 * NGX, 2 * LANES)
        field = nn_dot(rows, table).reshape(LEV, ROWS_DEV, 2 * LANES)
        for k in range(n, min(n + 2 * LANES, LON_DEV), LANES):
            width = min(LANES, LON_DEV - k)
            levels = [field[v, :, k - n : k - n + width] for v in range(LEV)]
            for p in range(POUT):
                below = bracket_v[p, :, k : k + width]
                weight = frac_v[p, :, k : k + width]
                low, high = two_levels(levels, below)
                out_ref[p, :, k : k + width] = (1.0 - weight) * low + weight * high

    wait_all(send1.at[pl.ds(0, NGX - 1)], send_sem.at[0])
    wait_all(send2.at[pl.ds(0, NGX - 1 - NYC * EARLY)], send_sem.at[1])
    for tz in range(EARLY):
        away = (tz - z) & (NZ - 1)
        is_far = jnp.abs(away - NZ // 2) <= FAR // 2

        @pl.when(is_far)
        def _():
            wait_all(far2.at[0, pl.ds(0, NX * NYC)], send_sem.at[3])

        @pl.when(jnp.logical_not(is_far))
        def _():
            wait_all(send2.at[pl.ds(0, NYC)], send_sem.at[1])

    wait_all(recv3.at[pl.ds(0, NX - 1)], send_sem.at[2])


def shards(fourier, lat_of_row, wave_order, analysis, synthesis, bracket, frac):
    lat = lat_of_row.reshape(LOOPS_DEV, LANES)
    wave = wave_order.reshape(1, WAVES)
    fourier = jnp.transpose(fourier, (1, 3, 2, 0))
    vmem = pl.BlockSpec(memory_space=pltpu.VMEM)
    hbm = pl.BlockSpec(memory_space=pltpu.HBM)
    return pl.pallas_call(
        kernel,
        out_shape=pltpu.VMEM((POUT, ROWS_DEV, LON_DEV), F32),
        in_specs=[hbm] * 7,
        out_specs=vmem,
        scratch_shapes=[
            pltpu.VMEM((2, LOOPS_DEV, LEV_DEV, WAVES), BF16),
            pltpu.VMEM((1, WAVES), I32),
            pltpu.VMEM((LOOPS_DEV, LANES), I32),
            pltpu.VMEM((WAVES, HALF), BF16),
            pltpu.VMEM((NGX * ROWS_DEV, WAVES), BF16),
            pltpu.VMEM((POUT, ROWS_DEV, LON_DEV), I32),
            pltpu.VMEM((POUT, ROWS_DEV, LON_DEV), F32),
            pltpu.VMEM((NGX, 2, LANES), BF16),
            pltpu.VMEM((NGX, 2, LANES), BF16),
            pltpu.VMEM((NGX, LANES), F32),
            pltpu.VMEM((NGX, LANES), F32),
            pltpu.VMEM((8 * ROWS_DEV, NGX), BF16),
            pltpu.VMEM((NX, 8 * ROWS_DEV, NGX), BF16),
            pltpu.VMEM((NX, NGX, LANES), F32),
            pltpu.VMEM((NX * 8 * ROWS_DEV, NGX), F32),
            pltpu.VMEM((LEV * ROWS_DEV, 2 * NGX), BF16),
            pltpu.VMEM((2, 24, LANES), I32),
            pltpu.VMEM((NLAT, WAVES), BF16),
            pltpu.VMEM((2 * NGX, LANES), F32),
            pltpu.VMEM((NGX * ROWS_DEV, WAVES), F32),
            pltpu.VMEM((NGX, ROWS_DEV * WAVES), BF16),
            pltpu.VMEM((WAVES, LANES), I32),
            pltpu.VMEM((2, NGX, LON_PAD), BF16),
            pltpu.VMEM((LEV, ROWS_DEV, LON_PAD), F32),
            pltpu.SemaphoreType.DMA((7,)),
            pltpu.SemaphoreType.DMA((4,)),
            pltpu.SemaphoreType.DMA((4,)),
        ],
        compiler_params=pltpu.CompilerParams(
            collective_id=0, has_side_effects=True, vmem_limit_bytes=56 * 1024 * 1024
        ),
        cost_estimate=pl.CostEstimate(flops=10**9, bytes_accessed=1400000, transcendentals=0),
    )(
        fourier, wave, lat, analysis.reshape(WAVES, HALF),
        synthesis.reshape(NGX * ROWS_DEV, WAVES), bracket, frac,
    )


def solution(mesh):
    placed = (
        P(None, None, "grp", "gx"),
        P(),
        P(),
        P("gx", None, None),
        P("gx", None, None),
        P(None, "gx", "grp"),
        P(None, "gx", "grp"),
    )
    return jax.shard_map(
        shards, mesh=mesh, in_specs=placed, out_specs=P(None, "gx", "grp"), check_vma=False
    )
```

```python
import functools
import math

import jax
import jax.numpy as jnp
from jax import lax
from jax.experimental import pallas as pl
from jax.experimental.pallas import tpu as pltpu
from jax.sharding import PartitionSpec as P

MESH = pl.DeviceIdType.MESH
F32, BF16, I32 = jnp.float32, jnp.bfloat16, jnp.int32

NX, NZ, NYC = 4, 16, 8
NGX = NZ * NYC
MTOT, NLAT, NLON = 1280, 2560, 3600
WAVES = 128
FIRST_WAVE = MTOT - WAVES
LEV_DEV, ROWS_DEV, LOOPS_DEV, LON_DEV, POUT, LEV = 4, 8, 20, 900, 8, 16
HALF = NLAT // 2
LANES = 128
LON_PAD = 1024
FIRST = 4
TABLE_SOON = 5
EARLY = 3
FAR = 5


def iota(shape, axis):
    return lax.broadcasted_iota(I32, shape, axis)


def nt_dot(a, b):
    return lax.dot_general(a, b, (((1,), (1,)), ((), ())), preferred_element_type=F32)


def nn_dot(a, b):
    return lax.dot_general(a, b, (((1,), (0,)), ((), ())), preferred_element_type=F32)


def ordered_waves(fourier, wave):
    pick = (iota((WAVES, WAVES), 0) == wave).astype(F32)
    pick = pick.T.astype(BF16)
    rows = jnp.concatenate([fourier[0].astype(F32), fourier[1].astype(F32)], axis=1)
    rows = rows.reshape(LOOPS_DEV * 8, WAVES)
    rows = jnp.concatenate([rows, jnp.zeros((256 - LOOPS_DEV * 8, WAVES), F32)], axis=0)
    return nt_dot(pick, rows.astype(BF16))


def loop_lats(lat):
    flat = iota((24, LANES), 1) * LOOPS_DEV + jnp.minimum(iota((24, LANES), 0), LOOPS_DEV - 1)
    high, low = flat >> 7, flat & (LANES - 1)
    out = jnp.zeros((24, LANES), I32)
    for a in range(LOOPS_DEV):
        row = jnp.broadcast_to(lat[a : a + 1], (24, LANES))
        out = jnp.where(high == a, jnp.take_along_axis(row, low, axis=1), out)
    return out


def table_tile(wave_col, lon):
    turns = wave_col * lon
    quarter = jnp.floor(turns.astype(F32) * (4.0 / NLON) + 0.5).astype(I32)
    rest = (turns - quarter * (NLON // 4)).astype(F32) * (2.0 * math.pi / NLON)
    sq = rest * rest
    c = 1.0 + sq * (-0.5 + sq * (1.0 / 24 + sq * (-1.0 / 720 + sq * (1.0 / 40320))))
    s = rest * (1.0 + sq * (-1.0 / 6 + sq * (1.0 / 120 + sq * (-1.0 / 5040 + sq * (1.0 / 362880)))))
    odd = (quarter & 1) == 1
    cos = jnp.where(odd, s, c)
    sin = jnp.where(odd, c, s)
    cos = jnp.where(((quarter + 1) & 2) == 2, -2.0 * cos, 2.0 * cos)
    sin = jnp.where((quarter & 2) == 2, 2.0 * sin, -2.0 * sin)
    return cos.astype(BF16), sin.astype(BF16)


def one_level(levels, bits):
    for bit in bits:
        levels = [jnp.where(bit, b, a) for a, b in zip(levels[0::2], levels[1::2])]
    return levels[0]


def two_levels(levels, below):
    bits = [(below & (1 << i)) != 0 for i in range(4)]

    def pair(values, bits):
        if not bits:
            return values[0], values[1]
        even, after = pair(values[0::2], bits[1:])
        odd = one_level(values[1::2], bits[1:])
        return jnp.where(bits[0], odd, even), jnp.where(bits[0], after, odd)

    return pair(levels + levels[-1:], bits)


def farthest_first(step, half):
    return half + ((step + 1) >> 1) * (1 - 2 * (step & 1))


def kernel(
    fourier_ref, wave_ref, lat_ref, analysis_ref, synthesis_ref, bracket_ref, frac_ref,
    out_ref,
    fourier_v, wave_v, lat_v, analysis_v, synthesis_v, bracket_v, frac_v,
    send1, recv1, send2, recv2, send3, recv3, far2, far_s, rows_s,
    lats_s, sorted_s, spread_s, syn_f, syn_s, wave_s, table_s, field_s,
    local_sem, send_sem, recv_sem,
):
    x = lax.axis_index("grp")
    gx = lax.axis_index("gx")
    z, yc = gx >> 3, gx & (NYC - 1)

    def near(tz, count, action):
        for j in range(count):
            action((tz << 3) + ((yc + farthest_first(j, NYC // 2)) & (NYC - 1)))

    def peers(action):
        @pl.loop(0, NZ - 1)
        def _(k):
            near((z + farthest_first(k, NZ // 2)) & (NZ - 1), NYC, action)

        near(z, NYC - 1, action)

    early = z < EARLY

    @pl.when(early)
    def _():
        recv2[...] = jnp.zeros((NGX, LANES), F32)
        far2[...] = jnp.zeros((NX, NGX, LANES), F32)

    barrier = pltpu.get_barrier_semaphore()

    def signal(tx, to):
        pl.semaphore_signal(barrier, inc=1, device_id=(tx, to), device_id_type=MESH)

    peers(lambda to: signal(x, to))
    for d in (2, 1, 3):
        signal((x + d) & (NX - 1), gx)

    local = [
        pltpu.make_async_copy(src, dst, local_sem.at[i])
        for i, (src, dst) in enumerate(
            (
                (fourier_ref, fourier_v),
                (wave_ref, wave_v),
                (lat_ref, lat_v),
                (analysis_ref, analysis_v),
                (synthesis_ref, synthesis_v),
                (bracket_ref, bracket_v),
                (frac_ref, frac_v),
            )
        )
    ]
    for copy in local:
        copy.start()

    def push(src, dst, stage, tx, to):
        pltpu.make_async_remote_copy(
            src_ref=src,
            dst_ref=dst,
            send_sem=send_sem.at[stage],
            recv_sem=recv_sem.at[stage],
            device_id=(tx, to),
            device_id_type=MESH,
        ).start()

    def wait_all(ref, sem):
        pltpu.make_async_copy(ref, ref, sem).wait()

    local[0].wait()
    local[1].wait()
    wave = wave_v[...]
    ordered = ordered_waves(fourier_v[...], wave)
    spread_s[pl.ds(0, NGX, stride=2), :] = ordered[:, :LANES]
    spread_s[pl.ds(1, NGX, stride=2), :] = ordered[:, LANES:]
    send1.reshape(2 * NGX, LANES)[...] = spread_s[...].astype(BF16)
    pl.semaphore_wait(barrier, NGX - 1 + NX - 1)
    peers(lambda to: push(send1.at[to], recv1.at[gx], 0, x, to))
    pltpu.make_async_copy(send1.at[gx], recv1.at[gx], recv_sem.at[0]).start()

    local[2].wait()
    lats = loop_lats(lat_v[...])
    own = jnp.sum(jnp.where(iota((1, WAVES), 1) == gx, wave, 0), axis=1, keepdims=True)
    pole = jnp.minimum(lats, NLAT - 1 - lats)
    live = 2 * (FIRST_WAVE + own) < 20 + 4 * pole
    lats_s[0] = jnp.where(live, pole, -1)
    lats_s[1] = jnp.where(lats >= HALF, 1, 0)
    local[3].wait()

    @pl.loop(0, LOOPS_DEV // 2)
    def _(pair):
        row = lats_s[0, pl.ds(2 * pair, 2), :]
        south = lats_s[1, pl.ds(2 * pair, 2), :]
        row = jnp.concatenate([row[0:1], row[1:2]], axis=1)
        south = jnp.concatenate([south[0:1], south[1:2]], axis=1)
        total = jnp.zeros((WAVES, 2 * LANES), F32)
        for j in range(0, HALF, 256):
            hot = (iota((256, 2 * LANES), 0) + j == row).astype(F32).astype(BF16)
            total += nn_dot(analysis_v[:, j : j + 256], hot)
        odd = iota((WAVES, 2 * LANES), 0) & 1
        total = jnp.where((odd * south) == 1, -total, total)
        sorted_s[pl.ds(pl.multiple_of(pair * 256, 256), 256), :] = total.T.astype(BF16)

    local[4].wait()
    syn_f[...] = synthesis_v[...].astype(F32)
    for ri in range(ROWS_DEV):
        syn_s[:, ri * LANES : (ri + 1) * LANES] = syn_f[pl.ds(ri, NGX, stride=ROWS_DEV), :].astype(BF16)

    wait_all(recv1, recv_sem.at[0])
    spread_s[...] = recv1.reshape(2 * NGX, LANES)[...].astype(F32)
    head = spread_s[pl.ds(0, NGX, stride=2), :].T
    tail = spread_s[pl.ds(1, NGX, stride=2), :].T
    loops = jnp.concatenate([head, tail], axis=0)
    loops = jnp.concatenate([loops[8 * s : 8 * s + 8] for s in range(LOOPS_DEV)], axis=1)
    spec = nn_dot(loops.astype(BF16), sorted_s[...])
    spec = jnp.where(iota((8, WAVES), 1) < WAVES - own, spec, 0.0).astype(BF16).astype(F32)
    wide = jnp.broadcast_to(spec[:, None, :], (8, ROWS_DEV, WAVES)).reshape(8 * ROWS_DEV, WAVES)
    ri = iota((8 * ROWS_DEV, WAVES), 0) & (ROWS_DEV - 1)
    wide = jnp.concatenate([jnp.where(ri == r, wide, 0.0) for r in range(ROWS_DEV)], axis=1)
    wide = jnp.concatenate([wide, wide], axis=0).astype(BF16)
    send2[...] = nt_dot(syn_s[...], wide).astype(BF16).astype(F32)

    def row_of(to):
        return send2.at[pl.ds(to, 1)]

    def push_row(to):
        push(row_of(to), recv2.at[pl.ds(gx, 1)], 1, x, to)

    def push_far(d, to):
        push(row_of(to), far2.at[x, pl.ds(gx, 1)], 3, (x + d) & (NX - 1), to)

    def push_plane(tz):
        is_far = jnp.abs(((tz - z) & (NZ - 1)) - NZ // 2) <= FAR // 2
        at_once = jnp.logical_and(is_far, tz < EARLY)

        @pl.when(at_once)
        def _():
            for d in (2, 1, 3, 0):
                near(tz, NYC, functools.partial(push_far, d))

        @pl.when(jnp.logical_and(jnp.logical_not(at_once), tz != z))
        def _():
            near(tz, NYC, push_row)

    pl.loop(0, FIRST)(push_plane)
    wave_s[...] = jnp.broadcast_to(wave.astype(F32), (WAVES, WAVES)).T.astype(I32) + FIRST_WAVE
    lon_start = x * LON_DEV

    def table_rows(i):
        at = pl.ds(pl.multiple_of(i * 16, 16), 16)
        col = wave_s[at, :]
        for n in range(0, LON_PAD, LANES):
            lon = iota((16, LANES), 1) + (lon_start + n)
            cos, sin = table_tile(col, lon)
            table_s[0, at, n : n + LANES] = cos
            table_s[1, at, n : n + LANES] = sin

    pl.loop(0, TABLE_SOON)(table_rows)
    pl.loop(FIRST, NZ)(push_plane)
    near(z, NYC - 1, push_row)
    pltpu.make_async_copy(row_of(gx), recv2.at[pl.ds(gx, 1)], recv_sem.at[1]).start()
    pl.loop(TABLE_SOON, NGX // 16)(table_rows)
    local[5].wait()
    local[6].wait()

    @pl.when(early)
    def _():
        wait_all(recv2.at[pl.ds(0, (NZ - FAR) * NYC)], recv_sem.at[1])

    @pl.when(jnp.logical_not(early))
    def _():
        wait_all(recv2, recv_sem.at[1])

    half = 4 * ROWS_DEV
    send3[...] = recv2[...].T[: 2 * half].astype(BF16)
    for d in (2, 1, 3):
        push(send3, recv3.at[x], 2, (x + d) & (NX - 1), gx)
    pltpu.make_async_copy(send3, recv3.at[x], recv_sem.at[2]).start()

    def set_rows(v, block):
        at = slice(v * half, (v + 1) * half)
        rows_s[at, :NGX] = block[:half]
        rows_s[at, NGX:] = block[half:]

    @pl.when(early)
    def _():
        wait_all(far2.at[:, pl.ds(0, FAR * NYC)], recv_sem.at[3])
        first = iota((NGX, LANES), 1) < 2 * half
        for v in range(0, NX, 2):
            both = jnp.where(first, far2[v], far2[v + 1]).T
            far_s[2 * half * v : 2 * half * (v + 2), :] = both
        wait_all(recv3, recv_sem.at[2])
        for v in range(NX):
            far = far_s[2 * half * v : 2 * half * (v + 1), :]
            set_rows(v, (recv3[v].astype(F32) + far).astype(BF16))

    @pl.when(jnp.logical_not(early))
    def _():
        wait_all(recv3, recv_sem.at[2])
        for v in range(NX):
            set_rows(v, recv3[v])

    rows = rows_s[...]
    for n in range(0, LON_DEV, 2 * LANES):
        table = table_s[:, :, n : n + 2 * LANES].reshape(2 * NGX, 2 * LANES)
        field = nn_dot(rows, table).reshape(LEV, ROWS_DEV, 2 * LANES)
        for k in range(n, min(n + 2 * LANES, LON_DEV), LANES):
            width = min(LANES, LON_DEV - k)
            levels = [field[v, :, k - n : k - n + width] for v in range(LEV)]
            for p in range(POUT):
                below = bracket_v[p, :, k : k + width]
                weight = frac_v[p, :, k : k + width]
                low, high = two_levels(levels, below)
                out_ref[p, :, k : k + width] = (1.0 - weight) * low + weight * high

    wait_all(send1.at[pl.ds(0, NGX - 1)], send_sem.at[0])
    wait_all(send2.at[pl.ds(0, NGX - 1 - NYC * EARLY)], send_sem.at[1])
    for tz in range(EARLY):
        away = (tz - z) & (NZ - 1)
        is_far = jnp.abs(away - NZ // 2) <= FAR // 2

        @pl.when(is_far)
        def _():
            wait_all(far2.at[0, pl.ds(0, NX * NYC)], send_sem.at[3])

        @pl.when(jnp.logical_not(is_far))
        def _():
            wait_all(send2.at[pl.ds(0, NYC)], send_sem.at[1])

    wait_all(recv3.at[pl.ds(0, NX - 1)], send_sem.at[2])


def shards(fourier, lat_of_row, wave_order, analysis, synthesis, bracket, frac):
    lat = lat_of_row.reshape(LOOPS_DEV, LANES)
    wave = wave_order.reshape(1, WAVES)
    fourier = jnp.transpose(fourier, (1, 3, 2, 0))
    vmem = pl.BlockSpec(memory_space=pltpu.VMEM)
    hbm = pl.BlockSpec(memory_space=pltpu.HBM)
    return pl.pallas_call(
        kernel,
        out_shape=pltpu.VMEM((POUT, ROWS_DEV, LON_DEV), F32),
        in_specs=[hbm] * 7,
        out_specs=vmem,
        scratch_shapes=[
            pltpu.VMEM((2, LOOPS_DEV, LEV_DEV, WAVES), BF16),
            pltpu.VMEM((1, WAVES), I32),
            pltpu.VMEM((LOOPS_DEV, LANES), I32),
            pltpu.VMEM((WAVES, HALF), BF16),
            pltpu.VMEM((NGX * ROWS_DEV, WAVES), BF16),
            pltpu.VMEM((POUT, ROWS_DEV, LON_DEV), I32),
            pltpu.VMEM((POUT, ROWS_DEV, LON_DEV), F32),
            pltpu.VMEM((NGX, 2, LANES), BF16),
            pltpu.VMEM((NGX, 2, LANES), BF16),
            pltpu.VMEM((NGX, LANES), F32),
            pltpu.VMEM((NGX, LANES), F32),
            pltpu.VMEM((8 * ROWS_DEV, NGX), BF16),
            pltpu.VMEM((NX, 8 * ROWS_DEV, NGX), BF16),
            pltpu.VMEM((NX, NGX, LANES), F32),
            pltpu.VMEM((NX * 8 * ROWS_DEV, NGX), F32),
            pltpu.VMEM((LEV * ROWS_DEV, 2 * NGX), BF16),
            pltpu.VMEM((2, 24, LANES), I32),
            pltpu.VMEM((NLAT, WAVES), BF16),
            pltpu.VMEM((2 * NGX, LANES), F32),
            pltpu.VMEM((NGX * ROWS_DEV, WAVES), F32),
            pltpu.VMEM((NGX, ROWS_DEV * WAVES), BF16),
            pltpu.VMEM((WAVES, LANES), I32),
            pltpu.VMEM((2, NGX, LON_PAD), BF16),
            pltpu.VMEM((LEV, ROWS_DEV, LON_PAD), F32),
            pltpu.SemaphoreType.DMA((7,)),
            pltpu.SemaphoreType.DMA((4,)),
            pltpu.SemaphoreType.DMA((4,)),
        ],
        compiler_params=pltpu.CompilerParams(
            collective_id=0, has_side_effects=True, vmem_limit_bytes=56 * 1024 * 1024
        ),
        cost_estimate=pl.CostEstimate(flops=10**9, bytes_accessed=1400000, transcendentals=0),
    )(
        fourier, wave, lat, analysis.reshape(WAVES, HALF),
        synthesis.reshape(NGX * ROWS_DEV, WAVES), bracket, frac,
    )


def solution(mesh):
    placed = (
        P(None, None, "grp", "gx"),
        P(),
        P(),
        P("gx", None, None),
        P("gx", None, None),
        P(None, "gx", "grp"),
        P(None, "gx", "grp"),
    )
    return jax.shard_map(
        shards, mesh=mesh, in_specs=placed, out_specs=P(None, "gx", "grp"), check_vma=False
    )
```
